32 devices in a mesh: grp: 4 (over x, core), exp: 8 (over z, y).
Axes of the slice: x: 2, y: 2, z: 4, core: 2. Of those that a mesh axis runs over, the one named last changes fastest.
Arguments:
- tokens: bfloat16 [4096, 2048], P(('grp', 'exp')), may hold values from -6 to 6
- grad_out: bfloat16 [4096, 2048], P(('grp', 'exp')), may hold values from -6 to 6
- probs: bfloat16 [4096, 6], P(('grp', 'exp')), may hold values from 0.049804688 to 0.3984375
- expert_ids: int32 [4096, 6], P(('grp', 'exp')), may hold values from 0 to 15, as said below
- serve_map: int32 [4, 8], replicated, may hold values from 0 to 1, as said below
- replica_pick: int32 [4096, 6], P(('grp', 'exp')), may hold values from 0 to 839
- w_gate: bfloat16 [16, 2048, 768], P('exp'), may hold values from -0.125 to 0.125
- w_up: bfloat16 [16, 2048, 768], P('exp'), may hold values from -0.125 to 0.125
- w_down: bfloat16 [16, 2048, 768], P('exp'), may hold values from -0.21875 to 0.21875
Outputs:
- grad_tokens: bfloat16 [4096, 2048], P(('grp', 'exp'))
- grad_probs: bfloat16 [4096, 6], P(('grp', 'exp'))
- grad_gate: float32 [16, 2048, 768], P('exp', 'grp')
- grad_up: float32 [16, 2048, 768], P('exp', 'grp')
- grad_down: float32 [16, 2048, 768], P('exp', 'grp')
The draws below stay inside these ranges and needn't reach their ends.
Inputs may be any that keep to these rules, and one draw needn't show every extreme that they name: `serve_map`: entry (g, c) names which of the experts c * 2 + entry the device of group g and column c serves; every expert is served by at least one group. `expert_ids`: each token names 6 different experts.
All inputs are finite; a program needn't handle non-finite values.
Results may differ from the reference program's by a relative error of at most 0.014.
Values may be sent and summed in bfloat16 or wider, within the bound.
No kernel may reach another device: no remote copies, remote signals or barrier semaphores. Data moves between devices by JAX's collectives and lax.ppermute only.
A program may use at most 128 MiB of HBM per device.

```python
import jax
import jax.numpy as jnp
from jax import lax

D = 2048
FF_WIN = 768
EXP_DEV = 2
TOPK = 6
TOK_DEV = 128
EXPERTS = 16
TOKENS = 4096
CAP = 32
N_GRP = 4
N_EXP = 8


def column_plan(key):
    base_key = jax.random.fold_in(key, 11)
    first_key, perm_key, noise_key = jax.random.split(base_key, 3)
    first_count = jax.random.randint(first_key, (N_EXP,), 1, N_GRP)
    perm_keys = jax.random.split(perm_key, N_EXP)
    position = jax.vmap(lambda sub_key: jax.random.permutation(sub_key, N_GRP))(perm_keys)
    serve = (position.T >= first_count[None, :]).astype(jnp.int32)
    noise_factor = jax.random.randint(noise_key, (N_EXP * EXP_DEV,), 1, 4)
    return (serve, noise_factor)


def draw_serve_map(key, part):
    serve, noise_factor = column_plan(key)
    return serve


def draw_expert_ids(key, part):
    serve, noise_factor = column_plan(key)
    members = jnp.arange(EXPERTS, dtype=jnp.int32) % EXP_DEV
    columns = jnp.arange(EXPERTS, dtype=jnp.int32) // EXP_DEV
    replica_count = jnp.sum((serve[:, columns] == members[None, :]).astype(jnp.int32), axis=0)
    weight = replica_count * noise_factor
    raw_scores = jax.random.randint(jax.random.fold_in(key, 23), (TOKENS, EXPERTS), 1, 1048576)
    scores = raw_scores * weight[None, :] * EXPERTS + jnp.arange(EXPERTS, dtype=jnp.int32)[None, :]
    return lax.top_k(scores, TOPK)[1].astype(jnp.int32)


def plant(values, rng, least, top_value):
    longest = values.shape.index(max(values.shape))
    spots = []
    for shift in (0, 1):
        where = [jax.random.randint(jax.random.fold_in(rng, axis), (), 0, length) for axis, length in enumerate(values.shape)]
        where[longest] = (where[longest] + shift) % values.shape[longest]
        spots.append(tuple(where))
    return values.at[spots[0]].set(least).at[spots[1]].set(top_value)


def block_levels(own_key, shape, pieces, low, largest):
    def one(dim, blocks):
        steps = jax.random.uniform(jax.random.fold_in(jax.random.fold_in(own_key, 6), dim), (blocks,), jnp.float32, low / len(pieces), largest / len(pieces))
        return jnp.repeat(jnp.exp(steps), shape[dim] // blocks).reshape((-1,) + (1,) * (len(shape) - dim - 1))

    loudness = one(*pieces[0])
    for cut in pieces[1:]:
        loudness = loudness * one(*cut)
    return loudness


def noise(key, dims, width, reach, shards=(), kind=jnp.bfloat16):
    entries = jax.random.normal(key, dims, jnp.float32) * width
    if len(shards) > 0:
        entries = block_levels(key, dims, shards, -0.22, 0.18) * entries
    return jnp.clip(entries, min=-reach, max=reach).astype(kind)


def setup_inputs(seed: int = 0) -> dict:
    splits = jax.random.split(jax.random.key(seed), 10)
    tokens = noise(splits[0], (TOKENS, D), 1.0, 6.0, ((0, 32),))
    grad_out = noise(splits[1], (TOKENS, D), 1.0, 6.0, ((0, 32),))
    probs = jnp.clip(0.049804688 + 0.3486328 * jax.random.uniform(splits[2], (TOKENS, TOPK), jnp.float32) ** block_levels(splits[2], (TOKENS, TOPK), ((0, 32),), -0.2, 0.2), 0.049804688, 0.3984375).astype(jnp.bfloat16)
    expert_ids = draw_expert_ids(jax.random.fold_in(splits[9], 71), 0)
    serve_map = draw_serve_map(jax.random.fold_in(splits[9], 71), 0)
    replica_pick = plant(jax.random.randint(splits[5], (TOKENS, TOPK), 0, 840), jax.random.fold_in(splits[5], 1), 0, 839).astype(jnp.int32)
    w_gate = noise(splits[6], (EXPERTS, D, FF_WIN), D ** -0.5, 0.125, ((0, 8),))
    w_up = noise(splits[7], (EXPERTS, D, FF_WIN), D ** -0.5, 0.125, ((0, 8),))
    w_down = noise(splits[8], (EXPERTS, D, FF_WIN), FF_WIN ** -0.5, 0.21875, ((0, 8),))
    return dict(tokens=tokens, grad_out=grad_out, probs=probs, expert_ids=expert_ids, serve_map=serve_map, replica_pick=replica_pick, w_gate=w_gate, w_up=w_up, w_down=w_down)


def route_targets(expert_ids, serve_map, replica_pick):
    groups = serve_map.shape[0]
    columns = serve_map.shape[1]
    column = expert_ids // EXP_DEV
    member = expert_ids % EXP_DEV
    serving = (serve_map[:, column] == member[None]).astype(jnp.int32)
    order_index = (jnp.cumsum(serving, axis=0) - 1).astype(jnp.int32)
    server_count = jnp.sum(serving, axis=0).astype(jnp.int32)
    wanted = (replica_pick % server_count).astype(jnp.int32)
    chosen_group = serving * (order_index == wanted[None]).astype(jnp.int32)
    group_index = jnp.sum(chosen_group * jnp.arange(groups, dtype=jnp.int32)[:, None, None], axis=0)
    return (group_index * columns + column).astype(jnp.int32)


def route_ranks(target_flat, devices):
    onehot = (target_flat[:, None] == jnp.arange(devices, dtype=jnp.int32)[None, :]).astype(jnp.int32)
    running = jnp.cumsum(onehot, axis=0) - onehot
    return jnp.sum(running * onehot, axis=1).astype(jnp.int32)


def expert_backward(input_rows, grad_rows, prob_rows, weight_gate, weight_up, weight_down):
    contract = (((1,), (1,)), ((), ()))
    over_rows = (((0,), (0,)), ((), ()))
    gate = jnp.dot(input_rows, weight_gate, preferred_element_type=jnp.float32)
    up_value = jnp.dot(input_rows, weight_up, preferred_element_type=jnp.float32)
    sigmoid_gate = jax.nn.sigmoid(gate)
    silu_gate = gate * sigmoid_gate
    hidden = (silu_gate * up_value).astype(jnp.bfloat16)
    output = lax.dot_general(hidden, weight_down, contract, preferred_element_type=jnp.float32)
    route_prob = jnp.sum(grad_rows.astype(jnp.float32) * output, axis=1).astype(jnp.bfloat16)
    scaled = (prob_rows.astype(jnp.float32)[:, None] * grad_rows.astype(jnp.float32)).astype(jnp.bfloat16)
    grad_hidden = jnp.dot(scaled, weight_down, preferred_element_type=jnp.float32)
    grad_gate_pre = (grad_hidden * up_value * sigmoid_gate * (1.0 + gate * (1.0 - sigmoid_gate))).astype(jnp.bfloat16)
    grad_up_pre = (grad_hidden * silu_gate).astype(jnp.bfloat16)
    route_grad = lax.dot_general(grad_gate_pre, weight_gate, contract, preferred_element_type=jnp.float32)
    route_grad = (route_grad + lax.dot_general(grad_up_pre, weight_up, contract, preferred_element_type=jnp.float32)).astype(jnp.bfloat16)
    part_gate = lax.dot_general(input_rows, grad_gate_pre, over_rows, preferred_element_type=jnp.float32).astype(jnp.bfloat16)
    part_up = lax.dot_general(input_rows, grad_up_pre, over_rows, preferred_element_type=jnp.float32).astype(jnp.bfloat16)
    part_down = lax.dot_general(scaled, hidden, over_rows, preferred_element_type=jnp.float32).astype(jnp.bfloat16)
    return route_grad, route_prob, part_gate, part_up, part_down


def reference(tokens, grad_out, probs, expert_ids, serve_map, replica_pick, w_gate, w_up, w_down):
    groups = serve_map.shape[0]
    columns = serve_map.shape[1]
    devices = groups * columns
    buffer_rows = devices * CAP
    target = route_targets(expert_ids, serve_map, replica_pick)
    blocks = target.reshape(devices, TOK_DEV * TOPK)
    slot_rank = jax.vmap(lambda block_targets: route_ranks(block_targets, devices))(blocks).reshape(TOKENS, TOPK)
    kept_mask = slot_rank < CAP
    route_id = jnp.arange(TOKENS * TOPK, dtype=jnp.int32).reshape(TOKENS, TOPK)
    source = route_id // (TOK_DEV * TOPK)
    send_slot = (target * buffer_rows + source * CAP + slot_rank).astype(jnp.int32)
    send_slot = jnp.where(kept_mask, send_slot, devices * buffer_rows).astype(jnp.int32)
    slot_table = jnp.full((devices * buffer_rows,), -1, jnp.int32)
    slot_table = slot_table.at[send_slot.reshape(-1)].set(route_id.reshape(-1), mode="drop")
    slot_table = slot_table.reshape(devices, buffer_rows)
    flat_probs = probs.reshape(-1)

    def one_device(running_sums, scan_entry):
        token_grad, prob_grad, sum_gate, sum_up, sum_down = running_sums
        device_index, slots = scan_entry
        live_mask = slots >= 0
        safe_slot = jnp.where(live_mask, slots, 0).astype(jnp.int32)
        token_row = (safe_slot // TOPK).astype(jnp.int32)
        input_rows = jnp.where(live_mask[:, None], tokens[token_row], jnp.zeros((), tokens.dtype))
        grad_rows = jnp.where(live_mask[:, None], grad_out[token_row], jnp.zeros((), grad_out.dtype))
        prob_rows = jnp.where(live_mask, flat_probs[safe_slot], jnp.zeros((), probs.dtype))
        group_index = device_index // columns
        column = device_index % columns
        expert = (column * EXP_DEV + serve_map[group_index, column]).astype(jnp.int32)
        route_grad, route_prob, part_gate, part_up, part_down = expert_backward(
            input_rows, grad_rows, prob_rows, w_gate[expert], w_up[expert], w_down[expert])
        token_target = jnp.where(live_mask, token_row, TOKENS).astype(jnp.int32)
        token_grad = token_grad.at[token_target].add(route_grad.astype(jnp.float32), mode="drop")
        prob_target = jnp.where(live_mask, safe_slot, TOKENS * TOPK).astype(jnp.int32)
        prob_grad = prob_grad.at[prob_target].set(route_prob, mode="drop")
        sum_gate = sum_gate.at[expert].add(part_gate.astype(jnp.float32))
        sum_up = sum_up.at[expert].add(part_up.astype(jnp.float32))
        sum_down = sum_down.at[expert].add(part_down.astype(jnp.float32))
        return (token_grad, prob_grad, sum_gate, sum_up, sum_down), None

    start = (jnp.zeros((TOKENS, D), jnp.float32), jnp.zeros((TOKENS * TOPK,), jnp.bfloat16),
             jnp.zeros((EXPERTS, D, FF_WIN), jnp.float32), jnp.zeros((EXPERTS, D, FF_WIN), jnp.float32),
             jnp.zeros((EXPERTS, D, FF_WIN), jnp.float32))
    final, unused = lax.scan(one_device, start, (jnp.arange(devices, dtype=jnp.int32), slot_table))
    token_grad, prob_grad, sum_gate, sum_up, sum_down = final
    return (token_grad.astype(jnp.bfloat16), prob_grad.reshape(TOKENS, TOPK), sum_gate, sum_up, sum_down)
```

```python
import functools

import jax
import jax.numpy as jnp
from jax import lax
from jax.experimental import pallas as pl
from jax.experimental.pallas import tpu as pltpu
from jax.sharding import PartitionSpec as P

EXP_DEV = 2
BF = jnp.bfloat16
F32 = jnp.float32


VMEM_BYTES = 56 * 2**20
ANY = pl.BlockSpec(memory_space=pl.ANY)


def dot(a, b, ca, cb):
    return lax.dot_general(a, b, (((ca,), (cb,)), ((), ())), preferred_element_type=F32)


def routing(probs, expert_ids, serve_map, replica_pick, capacity):
    groups, columns = serve_map.shape
    devices = groups * columns
    tokens = expert_ids.shape[0]
    member_of = serve_map.reshape(devices)
    serves_expert = 2 * (jnp.arange(devices, dtype=jnp.int32) % columns) + member_of
    same = (serve_map[:, None, :] == serve_map[None, :, :]).astype(jnp.int32)
    earlier = jnp.tril(jnp.ones((groups, groups), jnp.int32), -1)
    place = jnp.sum(same * earlier[:, :, None], axis=1).reshape(devices)
    count = jnp.sum(same, axis=1).reshape(devices)
    hit = (expert_ids[:, :, None] == serves_expert[None, None, :]) & (
        lax.rem(replica_pick[:, :, None], count[None, None, :]) == place[None, None, :]
    )
    chosen = jnp.sum(hit.astype(F32), axis=1)
    before = jnp.tril(jnp.ones((tokens, tokens), BF), -1)
    rank = dot(before, chosen.astype(BF), 1, 0)
    kept = (rank < capacity) & (chosen > 0)
    prob_dest = jnp.sum(jnp.where(hit, probs.astype(F32)[:, :, None], 0.0), axis=1)
    prob_dest = jnp.where(kept, prob_dest, 0.0).reshape(tokens, groups, columns)
    member = jnp.arange(EXP_DEV, dtype=jnp.int32)
    serving = (serve_map[:, :, None] == member[None, None, :]).astype(F32)
    prob_expert = jnp.sum(prob_dest[:, :, :, None] * serving[None], axis=1)
    kept_route = jnp.sum(jnp.where(hit & kept[:, None, :], 1.0, 0.0), axis=2) > 0
    return prob_expert, kept_route


def fetch(pieces, dst, sem, columns=None, at=0):
    copies = []
    row = 0
    for i, piece in enumerate(pieces):
        n = piece.shape[0]
        src = piece if columns is None else piece.at[:, columns]
        width = src.shape[1]
        copies.append(
            pltpu.make_async_copy(src, dst.at[pl.ds(row, n), pl.ds(at, width)], sem.at[i])
        )
        row += n
    for c in copies:
        c.start()
    return copies


def params(grid):
    return dict(
        compiler_params=pltpu.CompilerParams(
            vmem_limit_bytes=VMEM_BYTES, dimension_semantics=("arbitrary",) * grid
        )
    )


def cost(flops, nbytes, trans=0):
    return pl.CostEstimate(flops=int(flops), bytes_accessed=int(nbytes), transcendentals=int(trans))


def hidden_kernel(count, nb, *refs):
    pieces = refs[:count]
    wg, wu, hid, act, silu_out, x, sem = refs[count:]

    @pl.when(pl.program_id(0) == 0)
    def _():
        for c in fetch(pieces, x, sem):
            c.wait()

    for j in range(0, wg.shape[2], nb):
        cols = slice(j, j + nb)
        gate = jnp.dot(x[...], wg[0, :, cols], preferred_element_type=F32)
        up = jnp.dot(x[...], wu[0, :, cols], preferred_element_type=F32)
        sig = 1.0 / (1.0 + jnp.exp(-gate))
        silu = gate * sig
        hid[:, cols] = (silu * up).astype(BF)
        act[:, cols] = (up * sig * (1.0 + gate * (1.0 - sig))).astype(BF)
        silu_out[:, cols] = silu.astype(BF)


def hidden_call(pieces, w_gate, w_up, nb=256):
    rows = sum(a.shape[0] for a in pieces)
    n, width, ff = w_gate.shape
    ob = pl.BlockSpec((rows, ff), lambda m: (0, m))
    os = jax.ShapeDtypeStruct((rows, n * ff), BF)
    wb = pl.BlockSpec((1, width, ff), lambda m: (m, 0, 0))
    return pl.pallas_call(
        functools.partial(hidden_kernel, len(pieces), nb),
        grid=(n,),
        in_specs=[ANY] * len(pieces) + [wb, wb],
        out_specs=[ob] * 3,
        out_shape=[os] * 3,
        scratch_shapes=[pltpu.VMEM((rows, width), BF), pltpu.SemaphoreType.DMA((len(pieces),))],
        cost_estimate=cost(4 * rows * width * n * ff, 4 * n * width * ff + 8 * rows * ff * n),
        name="hidden",
        **params(1),
    )(*pieces, w_gate, w_up)


def back_kernel(counts, row_counts, planes, nb, plane_ref, *refs):
    na, nn = counts
    pa, pb = refs[:na], refs[na : na + nn]
    refs = refs[na + nn :]
    wd, p = refs[0], refs[1]
    k = len(row_counts)
    hid, act, silu = refs[2 : 2 + k], refs[2 + k : 2 + 2 * k], refs[2 + 2 * k : 2 + 3 * k]
    gg, gu, pg, g, sem, sem2 = refs[2 + 3 * k :]
    m = pl.program_id(0)
    w = g.shape[1] // planes

    @pl.when(m == 0)
    def _():
        one = fetch(pa, g, sem)
        two = fetch(pb, g, sem2, at=g.shape[1] - w)
        for c in one + two:
            c.wait()
        pg[...] = jnp.zeros_like(pg)

    row = 0
    for i, n in enumerate(row_counts):
        here = slice(row, row + n)
        pv = jnp.where(m == 0, p[here, 0:1], p[here, 1:2])
        total = jnp.zeros((n, 1), F32)
        for j in range(0, wd.shape[3], nb):
            cols = slice(j, j + nb)
            back = jnp.zeros((n, nb), F32)
            for s in range(planes):
                at = lax.rem(plane_ref[0] + 1 + s, planes)
                back += jnp.dot(
                    g[here, s * w : (s + 1) * w], wd[0, at, :, cols], preferred_element_type=F32
                )
            total += jnp.sum(back * hid[i][:, cols].astype(F32), axis=1, keepdims=True)
            back = back * pv
            gg[here, cols] = (back * act[i][:, cols]).astype(BF)
            gu[here, cols] = (back * silu[i][:, cols]).astype(BF)
        lane = lax.broadcasted_iota(jnp.int32, (n, pg.shape[1]), 1) == m
        pg[here, :] += jnp.where(lane, total, 0.0)
        row += n


def back_call(plane, pa, pb, w_down, p, hid, act, silu, planes, nb=256):
    rows = sum(a.shape[0] for a in pa)
    n, width, ff = w_down.shape
    w = width // planes
    row_counts = [a.shape[0] for a in hid]
    ob = pl.BlockSpec((rows, ff), lambda m, *_: (0, m))
    os = jax.ShapeDtypeStruct((rows, n * ff), BF)
    acts = [pl.BlockSpec((r, ff), lambda m, *_: (0, m)) for r in row_counts]
    wb = pl.BlockSpec((1, planes, w, ff), lambda m, *_: (m, 0, 0, 0))
    return pl.pallas_call(
        functools.partial(back_kernel, (len(pa), len(pb)), row_counts, planes, nb),
        grid_spec=pltpu.PrefetchScalarGridSpec(
            num_scalar_prefetch=1,
            grid=(n,),
            in_specs=[ANY] * (len(pa) + len(pb))
            + [wb, pl.BlockSpec((rows, n), lambda m, *_: (0, 0))]
            + acts * 3,
            out_specs=[ob, ob, pl.BlockSpec((rows, n), lambda m, *_: (0, 0))],
            scratch_shapes=[
                pltpu.VMEM((rows, width), BF),
                pltpu.SemaphoreType.DMA((len(pa),)),
                pltpu.SemaphoreType.DMA((len(pb),)),
            ],
        ),
        out_shape=[os, os, jax.ShapeDtypeStruct((rows, n), F32)],
        cost_estimate=cost(2 * rows * width * n * ff, 2 * n * width * ff + 14 * rows * ff * n),
        name="back",
        **params(1),
    )(plane, *pa, *pb, w_down.reshape(n, planes, w, ff), p, *hid, *act, *silu)


def part_kernel(count, row_counts, arrays, scale, start_ref, *refs):
    pieces = refs[:count]
    refs = refs[count:]
    if scale:
        p, refs = refs[0], refs[1:]
    k = len(row_counts)
    rhs = [refs[i * k : (i + 1) * k] for i in range(arrays)]
    refs = refs[arrays * k :]
    out, lhs, sem = refs
    block = lhs.shape[1]
    m = pl.program_id(0)

    @pl.when(m == 0)
    def _():
        cols = pl.ds(pl.multiple_of(start_ref[0] * 128, 128), block)
        for c in fetch(pieces, lhs, sem, columns=cols):
            c.wait()

    for i in range(arrays):
        total = None
        row = 0
        for j, n in enumerate(row_counts):
            r = rhs[i][j][...]
            if scale:
                here = slice(row, row + n)
                pv = jnp.where(m == 0, p[here, 0:1], p[here, 1:2])
                r = (r.astype(F32) * pv).astype(BF)
            t = lax.dot_general(
                lhs[row : row + n, :], r, (((0,), (0,)), ((), ())), preferred_element_type=F32
            )
            total = t if total is None else total + t
            row += n
        out[i, 0] = total.astype(BF)


def part_call(start, block, pieces, rhs, p=None):
    rows = sum(a.shape[0] for a in pieces)
    n = EXP_DEV
    k = len(rhs)
    ff = rhs[0][0].shape[1] // n
    row_counts = [a.shape[0] for a in rhs[0]]
    ob = pl.BlockSpec((k, 1, block, ff), lambda m, *_: (0, m, 0, 0))
    scale = [] if p is None else [p]
    flat_rhs = [a for r in rhs for a in r]
    return pl.pallas_call(
        functools.partial(part_kernel, len(pieces), row_counts, k, bool(scale)),
        grid_spec=pltpu.PrefetchScalarGridSpec(
            num_scalar_prefetch=1,
            grid=(n,),
            in_specs=[ANY] * len(pieces)
            + [pl.BlockSpec((rows, n), lambda m, *_: (0, 0))] * len(scale)
            + [pl.BlockSpec((r, ff), lambda m, *_: (0, m)) for r in row_counts] * k,
            out_specs=ob,
            scratch_shapes=[
                pltpu.VMEM((rows, block), BF),
                pltpu.SemaphoreType.DMA((len(pieces),)),
            ],
        ),
        out_shape=jax.ShapeDtypeStruct((k, n, block, ff), BF),
        cost_estimate=cost(
            2 * rows * block * n * ff * k,
            2 * rows * (block + k * n * ff) + 4 * k * n * block * ff,
        ),
        name="part",
        **params(1),
    )((start // 128).astype(jnp.int32).reshape(1), *pieces, *scale, *flat_rhs)


def input_kernel(gg, gu, wg, wu, out):
    ff = wg.shape[2]
    c = (((1,), (1,)), ((), ()))
    acc = lax.dot_general(gg[:, :ff], wg[0], c, preferred_element_type=F32)
    acc += lax.dot_general(gg[:, ff:], wg[1], c, preferred_element_type=F32)
    acc += lax.dot_general(gu[:, :ff], wu[0], c, preferred_element_type=F32)
    acc += lax.dot_general(gu[:, ff:], wu[1], c, preferred_element_type=F32)
    out[...] = acc.astype(BF)


def input_call(gg, gu, w_gate, w_up, nb=512):
    rows = gg.shape[0]
    n, width, ff = w_gate.shape
    wb = pl.BlockSpec((n, nb, ff), lambda j: (0, j, 0))
    gb = pl.BlockSpec((rows, n * ff), lambda j: (0, 0))
    return pl.pallas_call(
        input_kernel,
        grid=(width // nb,),
        in_specs=[gb, gb, wb, wb],
        out_specs=pl.BlockSpec((rows, nb), lambda j: (0, j)),
        out_shape=jax.ShapeDtypeStruct((rows, width), BF),
        cost_estimate=cost(
            4 * rows * width * n * ff, 4 * n * width * ff + 4 * rows * ff * n + 2 * rows * width
        ),
        name="input",
        **params(1),
    )(gg, gu, w_gate, w_up)


def after(a, *deps):
    return lax.optimization_barrier((a,) + deps)[0]


def body(tokens, grad_out, probs, expert_ids, serve_map, replica_pick, w_gate, w_up, w_down):
    groups = lax.axis_size("grp")
    columns = lax.axis_size("exp")
    devices = groups * columns
    planes = groups // 2
    half = columns // 2
    rows, width = tokens.shape
    top = expert_ids.shape[1]
    block = width // groups
    capacity = rows * top * 4 // (3 * devices)

    order = list(range(0, columns, 2)) + list(range(columns - 1, 0, -2))
    forward = [(order[i], order[(i + 1) % columns]) for i in range(columns)]
    backward = [(b, a) for a, b in forward]
    column = lax.axis_index("exp")
    position = jnp.where(column % 2 == 0, column // 2, columns - 1 - column // 2)
    offsets = [0]
    for s in range(1, half):
        offsets += [-s, s]
    offsets += [half]
    source = jnp.asarray(order, jnp.int32)[(position + jnp.asarray(offsets, jnp.int32)) % columns]

    def ring_step(s, f, b):
        if s < half:
            return lax.ppermute(f, "exp", forward), lax.ppermute(b, "exp", backward)
        h = f.shape[0] // 2
        return lax.ppermute(f[:h], "exp", forward), lax.ppermute(b[h:], "exp", backward)

    def tie(arrays, deps):
        n = len(arrays)
        return list(lax.optimization_barrier(tuple(arrays) + tuple(deps))[:n])

    def scatter_ring(a, waits):
        h = rows // 2
        at = {o: a[i * rows : (i + 1) * rows] for i, o in enumerate(offsets)}
        b, f = tie([at[half][:h], at[half][h:]], waits.get(1, []))
        b = lax.ppermute(b, "exp", backward)
        f = lax.ppermute(f, "exp", forward)
        for s in range(half - 1, 0, -1):
            mine_b, mine_f = at[-s].astype(F32), at[s].astype(F32)
            if s == half - 1:
                mine_b = jnp.concatenate([mine_b[:h] + b.astype(F32), mine_b[h:]], axis=0)
                mine_f = jnp.concatenate([mine_f[:h], mine_f[h:] + f.astype(F32)], axis=0)
            else:
                mine_b = mine_b + b.astype(F32)
                mine_f = mine_f + f.astype(F32)
            mine = [mine_b.astype(BF), mine_f.astype(BF)]
            mine_b, mine_f = tie(mine, waits.get(half + 1 - s, []))
            b = lax.ppermute(mine_b, "exp", backward)
            f = lax.ppermute(mine_f, "exp", forward)
        return (at[0].astype(F32) + b.astype(F32) + f.astype(F32)).astype(BF)

    group = lax.axis_index("grp")
    plane, core = group // 2, group % 2
    swap_core = [(g, g ^ 1) for g in range(groups)]

    w = width // planes
    doubled = jnp.concatenate([grad_out, grad_out], axis=1)
    rolled = lax.dynamic_slice_in_dim(doubled, (plane + 1) * w, width, axis=1)
    far, near = rolled[:, : width - w], rolled[:, width - w :]

    prob_expert, kept_route = routing(probs, expert_ids, serve_map, replica_pick, capacity)
    send = jnp.transpose(prob_expert, (1, 0, 2)).reshape(columns, rows * EXP_DEV).astype(BF)
    got = lax.all_to_all(send, "exp", split_axis=0, concat_axis=0, tiled=True)
    reorder = (source[:, None] == jnp.arange(columns, dtype=jnp.int32)[None, :]).astype(BF)
    prob_rows = dot(reorder, got, 1, 0).reshape(columns * rows, EXP_DEV)

    shift = {"x": 0, "far": 1, "near": half}
    first = {"x": tokens, "far": far, "near": near}
    arrived = {name: [a] for name, a in first.items()}
    hand = {name: [a, a] for name, a in first.items()}
    fresh = [tokens]
    hidden = []
    before = [send]
    for i in range(1, 2 * half + 1):
        names = [name for name in shift if 1 <= i - shift[name] <= half]
        moving = [a for name in names for a in hand[name]]
        if i > 1:
            moving = tie(moving, before)
        done = []
        for j, name in enumerate(names):
            hand[name] = ring_step(i - shift[name], *moving[2 * j : 2 * j + 2])
            arrived[name] += hand[name]
            done += hand[name]
            if name == "x":
                fresh += hand[name]
        before = done + (list(hidden[-1]) if i > 1 else [])
        if i == half:
            before += [prob_rows]
        if i < half - 1 or i == half:
            hidden.append(hidden_call(fresh, w_gate, w_up))
            fresh = []
    x_all, far_all, near_all = arrived["x"], arrived["far"], arrived["near"]
    hid, act, silu = [list(t) for t in zip(*hidden)]

    def part(s, lhs, which, rhs, p=None):
        start, pieces = lhs(s, which)
        return part_call(start, block, pieces, rhs, p)

    def to_core(a):
        return lax.ppermute(a, "grp", swap_core)

    def to_plane(s, a):
        return lax.ppermute(a, "grp", [(g, (g + 2 * s) % groups) for g in range(groups)])

    def of_x(s, which):
        return (((plane + s) % planes) * 2 + which) * block, x_all

    def of_far(s, which):
        return ((s - 1) * 2 + which) * block, far_all

    def of_near(s, which):
        return which * block, near_all

    def add(*arrays):
        return sum(a.astype(F32) for a in arrays)

    down = []
    free = []
    for s in range(1, planes):
        given = part(s, of_far, 1 - core, [hid], prob_rows)
        mine = part(s, of_far, core, [hid], prob_rows)
        got = to_core(given)
        for m in range(EXP_DEV):
            piece = add(mine[0, m], got[0, m]).astype(BF)
            if free:
                piece = after(piece, free[-1])
            else:
                plane_ref = after(plane.astype(jnp.int32).reshape(1), piece)
            free.append(to_plane(s, piece))
        down.append(free[-EXP_DEV:])

    gg, gu, prob_grad = back_call(
        plane_ref, far_all, near_all, w_down, prob_rows, hid, act, silu, planes
    )
    gg = after(gg, free[0])
    both = [[gg], [gu]]
    others = []
    chain = free[-1]
    for s in range(1, planes):
        given = part(s, of_x, 1 - core, both)
        mine = part(s, of_x, core, both)
        got = to_core(given)
        sums = []
        for i in range(2):
            for m in range(EXP_DEV):
                piece = add(mine[i, m], got[i, m]).astype(BF)
                chain = to_plane(s, after(piece, chain))
                sums.append(chain)
                if s == 1 and i == 0 and m == 0:
                    gg_x = after(gg, piece, free[-1])
        others.append(sums)
    first_sums = others[0]
    waits = {1: [first_sums[0]], half - 1: [first_sums[1]], half: [first_sums[2]]}
    grad_tokens = scatter_ring(input_call(gg_x, gu, w_gate, w_up), waits)

    given = part(0, of_x, 1 - core, both)
    mine = part(0, of_x, core, both)
    got = to_core(given)
    given_down = part(0, of_near, 1 - core, [hid], prob_rows)
    mine_down = part(0, of_near, core, [hid], prob_rows)
    got_down = to_core(given_down)

    def total(i, mine, got, theirs):
        return jnp.stack(
            [
                add(mine[i, m], got[i, m], *[t[i * EXP_DEV + m] for t in theirs])
                for m in range(EXP_DEV)
            ]
        )

    grad_down = total(0, mine_down, got_down, down)
    grad_gate = total(0, mine, got, others)
    grad_up = total(1, mine, got, others)

    ret = prob_grad.astype(BF).reshape(columns, rows * EXP_DEV)
    ret = dot(reorder, ret, 0, 0).astype(BF)
    ret = lax.all_to_all(ret, "exp", split_axis=0, concat_axis=0, tiled=True)
    ret = jnp.transpose(ret.reshape(columns, rows, EXP_DEV), (1, 0, 2)).reshape(rows, -1)
    pick = expert_ids[:, :, None] == jnp.arange(columns * EXP_DEV, dtype=jnp.int32)
    grad_probs = jnp.sum(jnp.where(pick, ret.astype(F32)[:, None, :], 0.0), axis=2)
    grad_probs = jnp.where(kept_route, grad_probs, 0.0).astype(BF)
    return (grad_tokens, grad_probs, grad_gate, grad_up, grad_down)


def solution(mesh):
    rows = P(("grp", "exp"), None)
    weights = P("exp", None, None)
    out = P("exp", "grp", None)
    return jax.shard_map(
        body,
        mesh=mesh,
        in_specs=(rows, rows, rows, rows, P(), rows, weights, weights, weights),
        out_specs=(rows, rows, out, out, out),
        check_vma=False,
    )
```

```python
import functools

import jax
import jax.numpy as jnp
from jax import lax
from jax.experimental import pallas as pl
from jax.experimental.pallas import tpu as pltpu
from jax.sharding import PartitionSpec as P

EXP_DEV = 2
BF = jnp.bfloat16
F32 = jnp.float32


VMEM_BYTES = 56 * 2**20
ANY = pl.BlockSpec(memory_space=pl.ANY)


def dot(a, b, ca, cb):
    return lax.dot_general(a, b, (((ca,), (cb,)), ((), ())), preferred_element_type=F32)


def routing(probs, expert_ids, serve_map, replica_pick, capacity):
    groups, columns = serve_map.shape
    devices = groups * columns
    tokens = expert_ids.shape[0]
    member_of = serve_map.reshape(devices)
    serves_expert = 2 * (jnp.arange(devices, dtype=jnp.int32) % columns) + member_of
    same = (serve_map[:, None, :] == serve_map[None, :, :]).astype(jnp.int32)
    earlier = jnp.tril(jnp.ones((groups, groups), jnp.int32), -1)
    place = jnp.sum(same * earlier[:, :, None], axis=1).reshape(devices)
    count = jnp.sum(same, axis=1).reshape(devices)
    hit = (expert_ids[:, :, None] == serves_expert[None, None, :]) & (
        lax.rem(replica_pick[:, :, None], count[None, None, :]) == place[None, None, :]
    )
    chosen = jnp.sum(hit.astype(F32), axis=1)
    before = jnp.tril(jnp.ones((tokens, tokens), BF), -1)
    rank = dot(before, chosen.astype(BF), 1, 0)
    kept = (rank < capacity) & (chosen > 0)
    prob_dest = jnp.sum(jnp.where(hit, probs.astype(F32)[:, :, None], 0.0), axis=1)
    prob_dest = jnp.where(kept, prob_dest, 0.0).reshape(tokens, groups, columns)
    member = jnp.arange(EXP_DEV, dtype=jnp.int32)
    serving = (serve_map[:, :, None] == member[None, None, :]).astype(F32)
    prob_expert = jnp.sum(prob_dest[:, :, :, None] * serving[None], axis=1)
    kept_route = jnp.sum(jnp.where(hit & kept[:, None, :], 1.0, 0.0), axis=2) > 0
    return prob_expert, kept_route


def fetch(pieces, dst, sem, columns=None, at=0):
    copies = []
    row = 0
    for i, piece in enumerate(pieces):
        n = piece.shape[0]
        src = piece if columns is None else piece.at[:, columns]
        width = src.shape[1]
        copies.append(
            pltpu.make_async_copy(src, dst.at[pl.ds(row, n), pl.ds(at, width)], sem.at[i])
        )
        row += n
    for c in copies:
        c.start()
    return copies


def params(grid):
    return dict(
        compiler_params=pltpu.CompilerParams(
            vmem_limit_bytes=VMEM_BYTES, dimension_semantics=("arbitrary",) * grid
        )
    )


def cost(flops, nbytes, trans=0):
    return pl.CostEstimate(flops=int(flops), bytes_accessed=int(nbytes), transcendentals=int(trans))


def hidden_kernel(count, nb, *refs):
    pieces = refs[:count]
    wg, wu, hid, act, silu_out, x, sem = refs[count:]

    @pl.when(pl.program_id(0) == 0)
    def _():
        for c in fetch(pieces, x, sem, columns=pl.ds(0, x.shape[1])):
            c.wait()

    for j in range(0, wg.shape[2], nb):
        cols = slice(j, j + nb)
        gate = jnp.dot(x[...], wg[0, :, cols], preferred_element_type=F32)
        up = jnp.dot(x[...], wu[0, :, cols], preferred_element_type=F32)
        sig = 1.0 / (1.0 + jnp.exp(-gate))
        silu = gate * sig
        hid[:, cols] = (silu * up).astype(BF)
        act[:, cols] = (up * sig * (1.0 + gate * (1.0 - sig))).astype(BF)
        silu_out[:, cols] = silu.astype(BF)


def hidden_call(pieces, w_gate, w_up, nb=256):
    rows = sum(a.shape[0] for a in pieces)
    n, width, ff = w_gate.shape
    ob = pl.BlockSpec((rows, ff), lambda m: (0, m))
    os = jax.ShapeDtypeStruct((rows, n * ff), BF)
    wb = pl.BlockSpec((1, width, ff), lambda m: (m, 0, 0))
    return pl.pallas_call(
        functools.partial(hidden_kernel, len(pieces), nb),
        grid=(n,),
        in_specs=[ANY] * len(pieces) + [wb, wb],
        out_specs=[ob] * 3,
        out_shape=[os] * 3,
        scratch_shapes=[pltpu.VMEM((rows, width), BF), pltpu.SemaphoreType.DMA((len(pieces),))],
        cost_estimate=cost(4 * rows * width * n * ff, 4 * n * width * ff + 8 * rows * ff * n),
        name="hidden",
        **params(1),
    )(*pieces, w_gate, w_up)


def back_kernel(counts, row_counts, late, planes, nb, plane_ref, *refs):
    na, nn = counts
    k = len(row_counts)
    pa, pb = refs[:na], refs[na : na + nn]
    refs = refs[na + nn :]
    acts = [refs[i * k : (i + 1) * k] for i in range(3)]
    wd, p = refs[3 * k : 3 * k + 2]
    gg0, gg1, gu0, gu1, pg, g, kept, sem, sem2, sem3 = refs[3 * k + 2 :]
    m = pl.program_id(0)
    w = g.shape[1] // planes
    ff = wd.shape[3]
    n_experts = kept.shape[2] // ff
    rest = g.shape[1] - w
    starts = [sum(row_counts[:i]) for i in range(k + 1)]
    chunks = [(0, k - late, gg0, gu0), (k - late, k, gg1, gu1)]

    def act_copies(lo, hi, e):
        cols = pl.ds(e * ff, ff)
        return [
            pltpu.make_async_copy(
                acts[t][i].at[:, cols],
                kept.at[t, pl.ds(starts[i], row_counts[i]), cols],
                sem3.at[t, i, e],
            )
            for i in range(lo, hi)
            for t in range(3)
        ]

    def row_copies(lo, hi):
        out = []
        row = 0
        for i in range(na):
            n = pa[i].shape[0]
            if starts[lo] <= row < starts[hi]:
                here = pl.ds(row, n)
                cols = pl.ds(pa[i].shape[1] - rest, rest)
                out.append(
                    pltpu.make_async_copy(
                        pa[i].at[:, cols], g.at[here, pl.ds(0, rest)], sem.at[i]
                    )
                )
                out.append(
                    pltpu.make_async_copy(pb[i], g.at[here, pl.ds(rest, w)], sem2.at[i])
                )
            row += n
        return out

    @pl.when(m == 0)
    def _():
        for lo, hi, _, _ in chunks:
            for c in row_copies(lo, hi) + act_copies(lo, hi, 0):
                c.start()
        for e in range(1, n_experts):
            for lo, hi, _, _ in chunks:
                for c in act_copies(lo, hi, e):
                    c.start()
        pg[...] = jnp.zeros_like(pg)

    for e in range(n_experts):

        @pl.when(m == e)
        def _(e=e):
            for lo, hi, gg, gu in chunks:
                waits = act_copies(lo, hi, e)
                if e == 0:
                    waits += row_copies(lo, hi)
                for c in waits:
                    c.wait()
                here = slice(starts[lo], starts[hi])
                n = starts[hi] - starts[lo]
                pv = p[here, e : e + 1]
                total = jnp.zeros((n, 1), F32)
                for j in range(0, ff, nb):
                    cols = slice(j, j + nb)
                    from_cols = slice(e * ff + j, e * ff + j + nb)
                    back = jnp.zeros((n, nb), F32)
                    for s in range(planes):
                        at = lax.rem(plane_ref[0] + 1 + s, planes)
                        back += jnp.dot(
                            g[here, s * w : (s + 1) * w],
                            wd[0, at, :, cols],
                            preferred_element_type=F32,
                        )
                    total += jnp.sum(
                        back * kept[0, here, from_cols].astype(F32), axis=1, keepdims=True
                    )
                    back = back * pv
                    gg[:, cols] = (back * kept[1, here, from_cols]).astype(BF)
                    gu[:, cols] = (back * kept[2, here, from_cols]).astype(BF)
                lane = lax.broadcasted_iota(jnp.int32, (n, pg.shape[1]), 1) == e
                pg[here, :] += jnp.where(lane, total, 0.0)


def back_call(plane, pa, pb, w_down, p, hid, act, silu, planes, late, nb=256):
    rows = sum(a.shape[0] for a in pa)
    n, width, ff = w_down.shape
    w = width // planes
    row_counts = [a.shape[0] for a in hid]
    k = len(row_counts)
    split = [sum(row_counts[: k - late]), sum(row_counts[k - late :])]
    ob = [pl.BlockSpec((r, ff), lambda m, *_: (0, m)) for r in split]
    os = [jax.ShapeDtypeStruct((r, n * ff), BF) for r in split]
    wb = pl.BlockSpec((1, planes, w, ff), lambda m, *_: (m, 0, 0, 0))
    return pl.pallas_call(
        functools.partial(back_kernel, (len(pa), len(pb)), row_counts, late, planes, nb),
        grid_spec=pltpu.PrefetchScalarGridSpec(
            num_scalar_prefetch=1,
            grid=(n,),
            in_specs=[ANY] * (len(pa) + len(pb) + 3 * k)
            + [wb, pl.BlockSpec((rows, n), lambda m, *_: (0, 0))],
            out_specs=ob + ob + [pl.BlockSpec((rows, n), lambda m, *_: (0, 0))],
            scratch_shapes=[
                pltpu.VMEM((rows, width), BF),
                pltpu.VMEM((3, rows, n * ff), BF),
                pltpu.SemaphoreType.DMA((len(pa),)),
                pltpu.SemaphoreType.DMA((len(pb),)),
                pltpu.SemaphoreType.DMA((3, k, n)),
            ],
        ),
        out_shape=os + os + [jax.ShapeDtypeStruct((rows, n), F32)],
        cost_estimate=cost(2 * rows * width * n * ff, 2 * n * width * ff + 14 * rows * ff * n),
        name="back",
        **params(1),
    )(plane, *pa, *pb, *hid, *act, *silu, w_down.reshape(n, planes, w, ff), p)


def part_kernel(count, row_counts, arrays, scale, sides, start_ref, *refs):
    pieces = refs[:count]
    refs = refs[count:]
    if scale:
        p, refs = refs[0], refs[1:]
    k = len(row_counts)
    rhs_in = [refs[i * k : (i + 1) * k] for i in range(arrays)]
    outs = refs[arrays * k : arrays * k + sides]
    lhs, rhs, sem, sem2 = refs[arrays * k + sides :]
    block = lhs.shape[2]
    ff = outs[0].shape[3]
    n_experts = rhs.shape[2] // ff
    m = pl.program_id(0)

    def rhs_copies(e):
        copies = []
        for i in range(arrays):
            row = 0
            for j, n in enumerate(row_counts):
                copies.append(
                    pltpu.make_async_copy(
                        rhs_in[i][j].at[:, pl.ds(e * ff, ff)],
                        rhs.at[i, pl.ds(row, n), pl.ds(e * ff, ff)],
                        sem2.at[i, j, e],
                    )
                )
                row += n
        return copies

    @pl.when(m == 0)
    def _():
        first = []
        for q in range(sides):
            cols = pl.ds(pl.multiple_of(start_ref[q] * 128, 128), block)
            first += fetch(pieces, lhs.at[q], sem.at[q], columns=cols)
        for e in range(n_experts):
            for c in rhs_copies(e):
                c.start()
        for c in first:
            c.wait()

    for e in range(n_experts):

        @pl.when(m == e)
        def _(e=e):
            for c in rhs_copies(e):
                c.wait()
            for i in range(arrays):
                r = rhs[i, :, e * ff : (e + 1) * ff]
                if scale:
                    r = r * p[:, e : e + 1].astype(BF)
                for q in range(sides):
                    outs[q][i, 0] = lax.dot_general(
                        lhs[q], r, (((0,), (0,)), ((), ())), preferred_element_type=F32
                    ).astype(BF)


def part_call(starts, block, pieces, rhs, p=None):
    sides = len(starts)
    rows = sum(a.shape[0] for a in pieces)
    n = EXP_DEV
    k = len(rhs)
    ff = rhs[0][0].shape[1] // n
    row_counts = [a.shape[0] for a in rhs[0]]
    scale = [] if p is None else [p]
    flat_rhs = [a for r in rhs for a in r]
    return pl.pallas_call(
        functools.partial(part_kernel, len(pieces), row_counts, k, bool(scale), sides),
        grid_spec=pltpu.PrefetchScalarGridSpec(
            num_scalar_prefetch=1,
            grid=(n,),
            in_specs=[ANY] * len(pieces)
            + [pl.BlockSpec((rows, n), lambda m, *_: (0, 0))] * len(scale)
            + [ANY] * len(flat_rhs),
            out_specs=[pl.BlockSpec((k, 1, block, ff), lambda m, *_: (0, m, 0, 0))] * sides,
            scratch_shapes=[
                pltpu.VMEM((sides, rows, block), BF),
                pltpu.VMEM((k, rows, n * ff), BF),
                pltpu.SemaphoreType.DMA((sides, len(pieces))),
                pltpu.SemaphoreType.DMA((k, len(row_counts), n)),
            ],
        ),
        out_shape=[jax.ShapeDtypeStruct((k, n, block, ff), BF)] * sides,
        cost_estimate=cost(
            2 * rows * block * n * ff * k * sides,
            2 * rows * (sides * block + k * n * ff) + 2 * sides * k * n * block * ff,
        ),
        name="part",
        **params(1),
    )(jnp.stack(starts).astype(jnp.int32) // 128, *pieces, *scale, *flat_rhs)


def input_kernel(first_row, column_ref, gg, gu, pg, wg, wu, out):
    ff = wg.shape[2]
    width = wg.shape[1] * pl.num_programs(0)
    c = (((1,), (1,)), ((), ()))
    acc = lax.dot_general(gg[:, :ff], wg[0], c, preferred_element_type=F32)
    acc += lax.dot_general(gg[:, ff:], wg[1], c, preferred_element_type=F32)
    acc += lax.dot_general(gu[:, :ff], wu[0], c, preferred_element_type=F32)
    acc += lax.dot_general(gu[:, ff:], wu[1], c, preferred_element_type=F32)
    nb = wg.shape[1]
    j = pl.program_id(0)
    out[:, pl.ds(pl.multiple_of(j * nb, nb), nb)] = acc.astype(BF)

    @pl.when(j == 0)
    def _():
        rows, extra = out.shape[0], out.shape[1] - width
        lane = lax.broadcasted_iota(jnp.int32, (rows, extra), 1)
        total = jnp.zeros((rows, extra), F32)
        for m in range(EXP_DEV):
            value = pg[first_row : first_row + rows, m : m + 1]
            total = jnp.where(lane == column_ref[0] * EXP_DEV + m, value, total)
        out[:, width:] = total.astype(BF)


def input_call(column, first_row, gg, gu, prob_grad, w_gate, w_up, extra, nb=512):
    rows = gg.shape[0]
    n, width, ff = w_gate.shape
    wb = pl.BlockSpec((n, nb, ff), lambda j, *_: (0, j, 0))
    gb = pl.BlockSpec((rows, n * ff), lambda j, *_: (0, 0))
    return pl.pallas_call(
        functools.partial(input_kernel, first_row),
        grid_spec=pltpu.PrefetchScalarGridSpec(
            num_scalar_prefetch=1,
            grid=(width // nb,),
            in_specs=[gb, gb, pl.BlockSpec(prob_grad.shape, lambda j, *_: (0, 0)), wb, wb],
            out_specs=pl.BlockSpec((rows, width + extra), lambda j, *_: (0, 0)),
        ),
        out_shape=jax.ShapeDtypeStruct((rows, width + extra), BF),
        cost_estimate=cost(
            4 * rows * width * n * ff, 4 * n * width * ff + 4 * rows * ff * n + 2 * rows * width
        ),
        name="input",
        **params(1),
    )(column, gg, gu, prob_grad, w_gate, w_up)


def finish_kernel(into, counts, *refs):
    refs = refs[into:]
    r = pl.program_id(0)
    total = refs[0][0, 0].astype(F32) + refs[1][0, 0].astype(F32)
    at = 2
    for n in counts:
        one = refs[at][...]
        for q in range(1, n):
            one = jnp.where(r == q, refs[at + q][...], one)
        total = total + one.astype(F32)
        at += n
    refs[-1][0] = total


def finish_call(i, m, mine, got, theirs, into=None, steps=2):
    _, n, block, ff = mine.shape
    rb = block // steps
    stacked = pl.BlockSpec((1, 1, rb, ff), lambda r: (i, m, r, 0))
    theirs = [t if isinstance(t, tuple) else (t,) for t in theirs]
    flat = []
    for t in theirs:
        if len(t) == 1:
            flat.append(pl.BlockSpec((rb, ff), lambda r: (r, 0)))
        else:
            flat += [pl.BlockSpec((rb, ff), lambda r: (0, 0))] * len(t)
    extra = [] if into is None else [into]
    return pl.pallas_call(
        functools.partial(finish_kernel, len(extra), [len(t) for t in theirs]),
        grid=(steps,),
        in_specs=[ANY] * len(extra) + [stacked, stacked] + flat,
        out_specs=pl.BlockSpec((1, rb, ff), lambda r: (m, r, 0)),
        out_shape=jax.ShapeDtypeStruct((n, block, ff), F32),
        input_output_aliases={0: 0} if extra else {},
        cost_estimate=cost(3 * block * ff, 10 * block * ff),
        name="finish",
        **params(1),
    )(*extra, mine, got, *[a for t in theirs for a in t])


def body(tokens, grad_out, probs, expert_ids, serve_map, replica_pick, w_gate, w_up, w_down):
    groups = lax.axis_size("grp")
    columns = lax.axis_size("exp")
    devices = groups * columns
    planes = groups // 2
    half = columns // 2
    rows, width = tokens.shape
    top = expert_ids.shape[1]
    block = width // groups
    capacity = rows * top * 4 // (3 * devices)

    order = list(range(0, columns, 2)) + list(range(columns - 1, 0, -2))
    forward = [(order[i], order[(i + 1) % columns]) for i in range(columns)]
    backward = [(b, a) for a, b in forward]
    column = lax.axis_index("exp")
    position = jnp.where(column % 2 == 0, column // 2, columns - 1 - column // 2)
    offsets = [0]
    for s in range(1, half):
        offsets += [-s, s]
    offsets += [half]
    source = jnp.asarray(order, jnp.int32)[(position + jnp.asarray(offsets, jnp.int32)) % columns]

    def ring_step(s, f, b):
        if s < half:
            return lax.ppermute(f, "exp", forward), lax.ppermute(b, "exp", backward)
        h = f.shape[0] // 2
        return lax.ppermute(f[:h], "exp", forward), lax.ppermute(b[h:], "exp", backward)

    def tie(arrays, deps):
        n = len(arrays)
        return list(lax.optimization_barrier(tuple(arrays) + tuple(deps))[:n])

    group = lax.axis_index("grp")
    plane, core = group // 2, group % 2
    swap_core = [(g, g ^ 1) for g in range(groups)]

    w = width // planes
    doubled = jnp.concatenate([grad_out, grad_out], axis=1)
    rolled = lax.dynamic_slice_in_dim(doubled, (plane + 1) * w, width, axis=1)
    far, near = rolled[:, : width - w], rolled[:, width - w :]

    def ready(a, deps):
        return tie([a], deps)[0]

    prob_expert, kept_route = routing(probs, expert_ids, serve_map, replica_pick, capacity)
    send = jnp.transpose(prob_expert, (1, 0, 2)).reshape(columns, rows * EXP_DEV).astype(BF)
    reorder = (source[:, None] == jnp.arange(columns, dtype=jnp.int32)[None, :]).astype(BF)

    def exchange(a):
        return lax.all_to_all(a, "exp", split_axis=0, concat_axis=0, tiled=True)

    shift = {"wide": 0, "near": half - 1}
    first = {"wide": jnp.concatenate([tokens, far], axis=1), "near": near}
    arrived = {name: [a] for name, a in first.items()}
    hand = {name: [a, a] for name, a in first.items()}
    fresh = [first["wide"]]
    hidden = []
    before = []
    stage_done = {}
    for i in range(1, half + 2):
        names = [name for name in shift if 1 <= i - shift[name] <= half]
        moving = [a for name in names for a in hand[name]]
        if before:
            moving = tie(moving, before)
        ran = []
        if i > 1:
            hidden.append(hidden_call(tie(fresh, before), w_gate, w_up))
            ran = list(hidden[-1])
            fresh = []
        if i == 3:
            prob_rows = dot(reorder, exchange(ready(send, before)), 1, 0)
            prob_rows = prob_rows.reshape(columns * rows, EXP_DEV)
            ran.append(prob_rows)
        done = []
        for j, name in enumerate(names):
            hand[name] = ring_step(i - shift[name], *moving[2 * j : 2 * j + 2])
            arrived[name] += hand[name]
            done += hand[name]
            if name == "wide":
                fresh += hand[name]
        before = done + ran + ([send] if i == 1 else [])
    x_all = arrived["wide"]
    hid, act, silu = [list(t) for t in zip(*hidden)]

    def near_step(s, before):
        hand["near"] = ring_step(s, *tie(hand["near"], before))
        arrived["near"] += hand["near"]
        return list(hand["near"])

    def part(s, lhs, which, rhs, p=None):
        start, pieces = lhs(s, which)
        return part_call([start], block, pieces, rhs, p)[0]

    def both_parts(lhs, rhs, p=None):
        (give_at, pieces), (keep_at, _) = lhs(0, 1 - core), lhs(0, core)
        return part_call([give_at, keep_at], block, pieces, rhs, p)

    def to_core(a):
        return lax.ppermute(a, "grp", swap_core)

    def to_plane(s, a):
        return lax.ppermute(a, "grp", [(g, (g + 2 * s) % groups) for g in range(groups)])

    def of_x(s, which):
        return (((plane + s) % planes) * 2 + which) * block, x_all

    def of_far(s, which):
        return width + ((s - 1) * 2 + which) * block, x_all

    def of_near(s, which):
        return which * block, near_all

    def add(*arrays):
        return sum(a.astype(F32) for a in arrays)

    given, mine, got = [], [], []
    for s in range(1, planes):
        hid_now = [ready(hid[0], before)] + hid[1:]
        given.append(part(s, of_far, 1 - core, [hid_now], prob_rows))
    done = near_step(3, before)
    before = done + given
    for s in range(1, planes):
        hid_now = [ready(hid[0], before)] + hid[1:]
        mine.append(part(s, of_far, core, [hid_now], prob_rows))
        got.append(to_core(ready(given[s - 1], before)))
    for s in range(4, half + 1):
        done = near_step(s, before if s == 4 else done)
    before = done + mine + got
    near_all = arrived["near"]

    sums = [add(mine[s - 1][0], got[s - 1][0]).astype(BF) for s in range(1, planes)]
    sums = tie(sums, done)
    h = block // 2

    def send_planes(cut, before):
        return [to_plane(s, ready(cut(sums[s - 1]), before)) for s in range(1, planes)]

    plane_ref = ready(plane.astype(jnp.int32).reshape(1), sums)
    gg0, gg1, gu0, gu1, prob_grad = back_call(
        plane_ref, x_all, near_all, w_down, prob_rows, hid, act, silu, planes, 2
    )
    down0 = send_planes(lambda a: a[0], done)
    gg0, gg1, gu0, gu1, *down0 = tie([gg0, gg1, gu0, gu1] + down0, [])
    both = [[gg0, gg1], [gu0, gu1]]
    given = [part(s, of_x, 1 - core, both) for s in range(1, planes)]
    down1 = send_planes(lambda a: a[1, :h], down0 + [gg0])
    gg0, *rest = tie([gg0] + given + down1, [])
    given, down1 = rest[: planes - 1], rest[planes - 1 :]
    both = [[gg0, gg1], [gu0, gu1]]
    mine = [part(s, of_x, core, both) for s in range(1, planes)]
    got = [to_core(a) for a in given]
    down2 = send_planes(lambda a: a[1, h:], down1 + given)
    gg0, *rest = tie([gg0] + mine + got + down2, [])
    mine, got, down2 = rest[: planes - 1], rest[planes - 1 : -(planes - 1)], rest[1 - planes :]
    down = [down0, list(zip(down1, down2))]

    sums = [add(a, b).astype(BF) for a, b in zip(mine, got)]
    cuts = [
        lambda a: a[0, 0, :h],
        lambda a: a[0, 0, h:],
        lambda a: a[0, 1],
        lambda a: a[1, 0],
        lambda a: a[1, 1],
    ]

    def send_piece(q, before):
        return send_planes(cuts[q], before)

    def step_back(b, f, before):
        b, f = tie([b, f], before)
        return lax.ppermute(b, "exp", backward), lax.ppermute(f, "exp", forward)

    sums = tie(sums, [])
    theirs = [send_piece(0, [])]
    extra = -(-columns * EXP_DEV // 128) * 128
    column_ref = column.astype(jnp.int32).reshape(1)
    cut = gg0.shape[0]
    late = input_call(
        column_ref, cut, ready(gg1, sums), gu1, prob_grad, w_gate, w_up, extra
    )
    late, gg0, *theirs[0] = tie([late, gg0] + theirs[0], [])
    at = {o: late[i * rows : (i + 1) * rows] for i, o in enumerate(offsets[-3:])}
    hr = rows // 2
    theirs.append(send_piece(1, [late]))
    b, f = step_back(at[half][:hr], at[half][hr:], [])
    rest = input_call(column_ref, 0, gg0, gu0, prob_grad, w_gate, w_up, extra)
    at.update({o: rest[i * rows : (i + 1) * rows] for i, o in enumerate(offsets[:-3])})
    before = theirs[1] + [b, f, rest]

    for s in range(half - 1, 0, -1):
        b, f, *before = tie([b, f] + before, [])
        mine_b, mine_f = at[-s], at[s]
        if s == half - 1:
            mine_b = jnp.concatenate([mine_b[:hr] + b, mine_b[hr:]], axis=0)
            mine_f = jnp.concatenate([mine_f[:hr], mine_f[hr:] + f], axis=0)
        else:
            mine_b = mine_b + b
            mine_f = mine_f + f
        b, f = step_back(mine_b, mine_f, before)
        done = [b, f]
        if len(theirs) < len(cuts):
            theirs.append(send_piece(len(theirs), before))
            done += theirs[-1]
        if s == half - 1:
            both = [[ready(gg0, before), gg1], [gu0, gu1]]
            give_x, keep_x = both_parts(of_x, both)
            done += [give_x, keep_x]
        if s == half - 2:
            hid_now = [ready(hid[0], before)] + hid[1:]
            give_n, keep_n = both_parts(of_near, [hid_now], prob_rows)
            got_x = to_core(ready(give_x, before))
            done += [give_n, keep_n, got_x]
        if s == half - 3:
            got_n = to_core(ready(give_n, before))
            gate0 = list(zip(theirs[0], theirs[1]))
            keep_x = ready(keep_x, before)
            grad_gate = finish_call(0, 0, keep_x, got_x, gate0)
            grad_gate = finish_call(0, 1, keep_x, got_x, theirs[2], grad_gate)
            grad_up = finish_call(1, 0, keep_x, got_x, theirs[3])
            grad_down = finish_call(0, 0, ready(keep_n, before), got_n, down[0])
            grad_down = finish_call(0, 1, keep_n, got_n, down[1], grad_down)
            done += [grad_gate, grad_up, grad_down]
        before = done
    back = (at[0].astype(F32) + b.astype(F32) + f.astype(F32)).astype(BF)
    grad_tokens, ret = back[:, :width], back[:, width : width + columns * EXP_DEV]
    keep_x = ready(keep_x, [grad_down, grad_gate, grad_up])
    grad_up = finish_call(1, 1, keep_x, got_x, theirs[4], grad_up)

    pick = expert_ids[:, :, None] == jnp.arange(columns * EXP_DEV, dtype=jnp.int32)
    grad_probs = jnp.sum(jnp.where(pick, ret.astype(F32)[:, None, :], 0.0), axis=2)
    grad_probs = jnp.where(kept_route, grad_probs, 0.0).astype(BF)
    return (grad_tokens, grad_probs, grad_gate, grad_up, grad_down)


def solution(mesh):
    rows = P(("grp", "exp"), None)
    weights = P("exp", None, None)
    out = P("exp", "grp", None)
    return jax.shard_map(
        body,
        mesh=mesh,
        in_specs=(rows, rows, rows, rows, P(), rows, weights, weights, weights),
        out_specs=(rows, rows, out, out, out),
        check_vma=False,
    )
```

```python
import functools

import jax
import jax.numpy as jnp
from jax import lax
from jax.experimental import pallas as pl
from jax.experimental.pallas import tpu as pltpu
from jax.sharding import PartitionSpec as P

EXP_DEV = 2
BF = jnp.bfloat16
F32 = jnp.float32


VMEM_BYTES = 56 * 2**20
ANY = pl.BlockSpec(memory_space=pl.ANY)


def dot(a, b, ca, cb):
    return lax.dot_general(a, b, (((ca,), (cb,)), ((), ())), preferred_element_type=F32)


def routing(probs, expert_ids, serve_map, replica_pick, capacity):
    groups, columns = serve_map.shape
    devices = groups * columns
    tokens = expert_ids.shape[0]
    member_of = serve_map.reshape(devices)
    serves_expert = 2 * (jnp.arange(devices, dtype=jnp.int32) % columns) + member_of
    same = (serve_map[:, None, :] == serve_map[None, :, :]).astype(jnp.int32)
    earlier = jnp.tril(jnp.ones((groups, groups), jnp.int32), -1)
    place = jnp.sum(same * earlier[:, :, None], axis=1).reshape(devices)
    count = jnp.sum(same, axis=1).reshape(devices)
    hit = (expert_ids[:, :, None] == serves_expert[None, None, :]) & (
        lax.rem(replica_pick[:, :, None], count[None, None, :]) == place[None, None, :]
    )
    chosen = jnp.sum(hit.astype(F32), axis=1)
    before = jnp.tril(jnp.ones((tokens, tokens), BF), -1)
    rank = dot(before, chosen.astype(BF), 1, 0)
    kept = (rank < capacity) & (chosen > 0)
    prob_dest = jnp.sum(jnp.where(hit, probs.astype(F32)[:, :, None], 0.0), axis=1)
    prob_dest = jnp.where(kept, prob_dest, 0.0).reshape(tokens, groups, columns)
    member = jnp.arange(EXP_DEV, dtype=jnp.int32)
    serving = (serve_map[:, :, None] == member[None, None, :]).astype(F32)
    prob_expert = jnp.sum(prob_dest[:, :, :, None] * serving[None], axis=1)
    kept_route = jnp.sum(jnp.where(hit & kept[:, None, :], 1.0, 0.0), axis=2) > 0
    return prob_expert, kept_route


def fetch(pieces, dst, sem, columns=None, at=0):
    copies = []
    row = 0
    for i, piece in enumerate(pieces):
        n = piece.shape[0]
        src = piece if columns is None else piece.at[:, columns]
        width = src.shape[1]
        copies.append(
            pltpu.make_async_copy(src, dst.at[pl.ds(row, n), pl.ds(at, width)], sem.at[i])
        )
        row += n
    for c in copies:
        c.start()
    return copies


def params(grid, nbytes):
    return dict(
        compiler_params=pltpu.CompilerParams(
            vmem_limit_bytes=min(VMEM_BYTES, int(nbytes) + 10 * 2**20),
            dimension_semantics=("arbitrary",) * grid,
        )
    )


def cost(flops, nbytes, trans=0):
    return pl.CostEstimate(flops=int(flops), bytes_accessed=int(nbytes), transcendentals=int(trans))


def hidden_kernel(count, nb, *refs):
    pieces = refs[:count]
    wg, wu, hid, act, silu_out, x, sem = refs[count:]

    @pl.when(pl.program_id(0) == 0)
    def _():
        for c in fetch(pieces, x, sem, columns=pl.ds(0, x.shape[1])):
            c.wait()

    for j in range(0, wg.shape[2], nb):
        cols = slice(j, j + nb)
        gate = jnp.dot(x[...], wg[0, :, cols], preferred_element_type=F32)
        up = jnp.dot(x[...], wu[0, :, cols], preferred_element_type=F32)
        sig = 1.0 / (1.0 + jnp.exp(-gate))
        silu = gate * sig
        hid[:, cols] = (silu * up).astype(BF)
        act[:, cols] = (up * sig * (1.0 + gate * (1.0 - sig))).astype(BF)
        silu_out[:, cols] = silu.astype(BF)


def hidden_call(pieces, w_gate, w_up, nb=256):
    rows = sum(a.shape[0] for a in pieces)
    n, width, ff = w_gate.shape
    ob = pl.BlockSpec((rows, ff), lambda m: (0, m))
    os = jax.ShapeDtypeStruct((rows, n * ff), BF)
    wb = pl.BlockSpec((1, width, ff), lambda m: (m, 0, 0))
    return pl.pallas_call(
        functools.partial(hidden_kernel, len(pieces), nb),
        grid=(n,),
        in_specs=[ANY] * len(pieces) + [wb, wb],
        out_specs=[ob] * 3,
        out_shape=[os] * 3,
        scratch_shapes=[pltpu.VMEM((rows, width), BF), pltpu.SemaphoreType.DMA((len(pieces),))],
        cost_estimate=cost(4 * rows * width * n * ff, 4 * n * width * ff + 8 * rows * ff * n),
        name="hidden",
        **params(1, VMEM_BYTES),
    )(*pieces, w_gate, w_up)


def back_kernel(counts, row_counts, late, planes, nb, plane_ref, *refs):
    na, nn = counts
    k = len(row_counts)
    pa, pb = refs[:na], refs[na : na + nn]
    refs = refs[na + nn :]
    acts = [refs[i * k : (i + 1) * k] for i in range(3)]
    wd, p = refs[3 * k : 3 * k + 2]
    gg0, gg1, gu0, gu1, pg, g, kept, sem, sem2, sem3 = refs[3 * k + 2 :]
    m = pl.program_id(0)
    w = g.shape[1] // planes
    ff = wd.shape[3]
    n_experts = kept.shape[2] // ff
    rest = g.shape[1] - w
    starts = [sum(row_counts[:i]) for i in range(k + 1)]
    chunks = [(0, k - late, gg0, gu0), (k - late, k, gg1, gu1)]

    def act_copies(lo, hi, e):
        cols = pl.ds(e * ff, ff)
        return [
            pltpu.make_async_copy(
                acts[t][i].at[:, cols],
                kept.at[t, pl.ds(starts[i], row_counts[i]), cols],
                sem3.at[t, i, e],
            )
            for i in range(lo, hi)
            for t in range(3)
        ]

    def row_copies(lo, hi):
        out = []
        row = 0
        for i in range(na):
            n = pa[i].shape[0]
            if starts[lo] <= row < starts[hi]:
                here = pl.ds(row, n)
                cols = pl.ds(pa[i].shape[1] - rest, rest)
                out.append(
                    pltpu.make_async_copy(
                        pa[i].at[:, cols], g.at[here, pl.ds(0, rest)], sem.at[i]
                    )
                )
                out.append(
                    pltpu.make_async_copy(pb[i], g.at[here, pl.ds(rest, w)], sem2.at[i])
                )
            row += n
        return out

    @pl.when(m == 0)
    def _():
        for lo, hi, _, _ in chunks:
            for c in row_copies(lo, hi) + act_copies(lo, hi, 0):
                c.start()
        for e in range(1, n_experts):
            for lo, hi, _, _ in chunks:
                for c in act_copies(lo, hi, e):
                    c.start()
        pg[...] = jnp.zeros_like(pg)

    for e in range(n_experts):

        @pl.when(m == e)
        def _(e=e):
            for lo, hi, gg, gu in chunks:
                waits = act_copies(lo, hi, e)
                if e == 0:
                    waits += row_copies(lo, hi)
                for c in waits:
                    c.wait()
                here = slice(starts[lo], starts[hi])
                n = starts[hi] - starts[lo]
                pv = p[here, e : e + 1]
                total = jnp.zeros((n, 1), F32)
                for j in range(0, ff, nb):
                    cols = slice(j, j + nb)
                    from_cols = slice(e * ff + j, e * ff + j + nb)
                    back = jnp.zeros((n, nb), F32)
                    for s in range(planes):
                        at = lax.rem(plane_ref[0] + 1 + s, planes)
                        back += jnp.dot(
                            g[here, s * w : (s + 1) * w],
                            wd[0, at, :, cols],
                            preferred_element_type=F32,
                        )
                    total += jnp.sum(
                        back * kept[0, here, from_cols].astype(F32), axis=1, keepdims=True
                    )
                    back = (back * pv).astype(BF)
                    gg[:, cols] = back * kept[1, here, from_cols]
                    gu[:, cols] = back * kept[2, here, from_cols]
                lane = lax.broadcasted_iota(jnp.int32, (n, pg.shape[1]), 1) == e
                pg[here, :] += jnp.where(lane, total, 0.0)


def back_call(plane, pa, pb, w_down, p, hid, act, silu, planes, late, nb=256):
    rows = sum(a.shape[0] for a in pa)
    n, width, ff = w_down.shape
    w = width // planes
    row_counts = [a.shape[0] for a in hid]
    k = len(row_counts)
    split = [sum(row_counts[: k - late]), sum(row_counts[k - late :])]
    ob = [pl.BlockSpec((r, ff), lambda m, *_: (0, m)) for r in split]
    os = [jax.ShapeDtypeStruct((r, n * ff), BF) for r in split]
    wb = pl.BlockSpec((1, planes, w, ff), lambda m, *_: (m, 0, 0, 0))
    return pl.pallas_call(
        functools.partial(back_kernel, (len(pa), len(pb)), row_counts, late, planes, nb),
        grid_spec=pltpu.PrefetchScalarGridSpec(
            num_scalar_prefetch=1,
            grid=(n,),
            in_specs=[ANY] * (len(pa) + len(pb) + 3 * k)
            + [wb, pl.BlockSpec((rows, n), lambda m, *_: (0, 0))],
            out_specs=ob + ob + [pl.BlockSpec((rows, n), lambda m, *_: (0, 0))],
            scratch_shapes=[
                pltpu.VMEM((rows, width), BF),
                pltpu.VMEM((3, rows, n * ff), BF),
                pltpu.SemaphoreType.DMA((len(pa),)),
                pltpu.SemaphoreType.DMA((len(pb),)),
                pltpu.SemaphoreType.DMA((3, k, n)),
            ],
        ),
        out_shape=os + os + [jax.ShapeDtypeStruct((rows, n), F32)],
        cost_estimate=cost(2 * rows * width * n * ff, 2 * n * width * ff + 14 * rows * ff * n),
        name="back",
        **params(1, VMEM_BYTES),
    )(plane, *pa, *pb, *hid, *act, *silu, w_down.reshape(n, planes, w, ff), p)


def part_kernel(count, row_counts, arrays, scale, sides, start_ref, *refs):
    pieces = refs[:count]
    refs = refs[count:]
    if scale:
        p, refs = refs[0], refs[1:]
    k = len(row_counts)
    rhs_in = [refs[i * k : (i + 1) * k] for i in range(arrays)]
    outs = refs[arrays * k : arrays * k + sides]
    lhs, rhs, sem, sem2 = refs[arrays * k + sides :]
    block = lhs.shape[2]
    ff = outs[0].shape[3]
    n_experts = rhs.shape[2] // ff
    m = pl.program_id(0)

    def rhs_copies(e):
        copies = []
        for i in range(arrays):
            row = 0
            for j, n in enumerate(row_counts):
                copies.append(
                    pltpu.make_async_copy(
                        rhs_in[i][j].at[:, pl.ds(e * ff, ff)],
                        rhs.at[i, pl.ds(row, n), pl.ds(e * ff, ff)],
                        sem2.at[i, j, e],
                    )
                )
                row += n
        return copies

    @pl.when(m == 0)
    def _():
        first = []
        for q in range(sides):
            cols = pl.ds(pl.multiple_of(start_ref[q] * 128, 128), block)
            first += fetch(pieces, lhs.at[q], sem.at[q], columns=cols)
        for e in range(n_experts):
            for c in rhs_copies(e):
                c.start()
        for c in first:
            c.wait()

    for e in range(n_experts):

        @pl.when(m == e)
        def _(e=e):
            for c in rhs_copies(e):
                c.wait()
            for i in range(arrays):
                r = rhs[i, :, e * ff : (e + 1) * ff]
                if scale:
                    r = r * p[:, e : e + 1].astype(BF)
                for q in range(sides):
                    outs[q][i, 0] = lax.dot_general(
                        lhs[q], r, (((0,), (0,)), ((), ())), preferred_element_type=F32
                    ).astype(BF)


def part_call(starts, block, pieces, rhs, p=None):
    sides = len(starts)
    rows = sum(a.shape[0] for a in pieces)
    n = EXP_DEV
    k = len(rhs)
    ff = rhs[0][0].shape[1] // n
    row_counts = [a.shape[0] for a in rhs[0]]
    scale = [] if p is None else [p]
    flat_rhs = [a for r in rhs for a in r]
    nbytes = 2 * rows * (sides * block + k * n * ff) + 4 * sides * k * block * ff
    nbytes += 8 * block * ff + 1024 * rows
    return pl.pallas_call(
        functools.partial(part_kernel, len(pieces), row_counts, k, bool(scale), sides),
        grid_spec=pltpu.PrefetchScalarGridSpec(
            num_scalar_prefetch=1,
            grid=(n,),
            in_specs=[ANY] * len(pieces)
            + [pl.BlockSpec((rows, n), lambda m, *_: (0, 0))] * len(scale)
            + [ANY] * len(flat_rhs),
            out_specs=[pl.BlockSpec((k, 1, block, ff), lambda m, *_: (0, m, 0, 0))] * sides,
            scratch_shapes=[
                pltpu.VMEM((sides, rows, block), BF),
                pltpu.VMEM((k, rows, n * ff), BF),
                pltpu.SemaphoreType.DMA((sides, len(pieces))),
                pltpu.SemaphoreType.DMA((k, len(row_counts), n)),
            ],
        ),
        out_shape=[jax.ShapeDtypeStruct((k, n, block, ff), BF)] * sides,
        cost_estimate=cost(
            2 * rows * block * n * ff * k * sides,
            2 * rows * (sides * block + k * n * ff) + 2 * sides * k * n * block * ff,
        ),
        name="part",
        **params(1, nbytes if sides > 1 else VMEM_BYTES),
    )(jnp.stack(starts).astype(jnp.int32) // 128, *pieces, *scale, *flat_rhs)


def input_kernel(first_row, column_ref, gg, gu, pg, wg, wu, out):
    ff = wg.shape[2]
    width = wg.shape[1] * pl.num_programs(0)
    c = (((1,), (1,)), ((), ()))
    acc = lax.dot_general(gg[:, :ff], wg[0], c, preferred_element_type=F32)
    acc += lax.dot_general(gg[:, ff:], wg[1], c, preferred_element_type=F32)
    acc += lax.dot_general(gu[:, :ff], wu[0], c, preferred_element_type=F32)
    acc += lax.dot_general(gu[:, ff:], wu[1], c, preferred_element_type=F32)
    nb = wg.shape[1]
    j = pl.program_id(0)
    out[:, pl.ds(pl.multiple_of(j * nb, nb), nb)] = acc.astype(BF)

    @pl.when(j == 0)
    def _():
        rows, extra = out.shape[0], out.shape[1] - width
        lane = lax.broadcasted_iota(jnp.int32, (rows, extra), 1)
        total = jnp.zeros((rows, extra), F32)
        for m in range(EXP_DEV):
            value = pg[first_row : first_row + rows, m : m + 1]
            total = jnp.where(lane == column_ref[0] * EXP_DEV + m, value, total)
        out[:, width:] = total.astype(BF)


def input_call(column, first_row, gg, gu, prob_grad, w_gate, w_up, extra, ahead, nb=512):
    rows = gg.shape[0]
    n, width, ff = w_gate.shape
    wb = pl.BlockSpec((n, nb, ff), lambda j, *_: (0, j, 0))
    gb = pl.BlockSpec((rows, n * ff), lambda j, *_: (0, 0))
    nbytes = 4 * (2 * rows * n * ff + rows * (width + extra) + 2 * n * nb * ff) + 8 * rows * nb
    return pl.pallas_call(
        functools.partial(input_kernel, first_row),
        grid_spec=pltpu.PrefetchScalarGridSpec(
            num_scalar_prefetch=1,
            grid=(width // nb,),
            in_specs=[gb, gb, pl.BlockSpec(prob_grad.shape, lambda j, *_: (0, 0)), wb, wb],
            out_specs=pl.BlockSpec((rows, width + extra), lambda j, *_: (0, 0)),
        ),
        out_shape=jax.ShapeDtypeStruct((rows, width + extra), BF),
        cost_estimate=cost(
            4 * rows * width * n * ff, 4 * n * width * ff + 4 * rows * ff * n + 2 * rows * width
        ),
        name="input",
        **params(1, nbytes if ahead else VMEM_BYTES),
    )(column, gg, gu, prob_grad, w_gate, w_up)


def finish_kernel(into, counts, steps, *refs):
    refs = refs[into:]
    rb = refs[-1].shape[1]
    r = pl.program_id(0)

    for k in range(steps):

        @pl.when(r == k)
        def _(k=k):
            total = refs[0][0, 0].astype(F32) + refs[1][0, 0].astype(F32)
            at = 2
            for sizes in counts:
                rows, row = [], 0
                for n in sizes:
                    lo, hi = max(row, k * rb), min(row + n, (k + 1) * rb)
                    if lo < hi:
                        rows.append(refs[at][lo - row : hi - row])
                    row += n
                    at += 1
                one = rows[0] if len(rows) == 1 else jnp.concatenate(rows, axis=0)
                total = total + one.astype(F32)
            refs[-1][0] = total


def finish_call(i, m, mine, got, theirs, into=None, last=False, steps=2):
    _, n, block, ff = mine.shape
    rb = block // steps
    stacked = pl.BlockSpec((1, 1, rb, ff), lambda r: (i, m, r, 0))
    extra = [] if into is None else [into]
    arrays = [a for t in theirs for a in t]
    return pl.pallas_call(
        functools.partial(
            finish_kernel, len(extra), [[a.shape[0] for a in t] for t in theirs], steps
        ),
        grid=(steps,),
        in_specs=[ANY] * len(extra)
        + [stacked, stacked]
        + [pl.BlockSpec(a.shape, lambda r: (0, 0)) for a in arrays],
        out_specs=pl.BlockSpec((1, rb, ff), lambda r: (m, r, 0)),
        out_shape=jax.ShapeDtypeStruct((n, block, ff), F32),
        input_output_aliases={0: 0} if extra else {},
        cost_estimate=cost(3 * block * ff, 10 * block * ff),
        name="finish",
        **params(1, VMEM_BYTES if last else 24 * block * ff),
    )(*extra, mine, got, *arrays)


def body(tokens, grad_out, probs, expert_ids, serve_map, replica_pick, w_gate, w_up, w_down):
    groups = lax.axis_size("grp")
    columns = lax.axis_size("exp")
    devices = groups * columns
    planes = groups // 2
    half = columns // 2
    rows, width = tokens.shape
    top = expert_ids.shape[1]
    block = width // groups
    capacity = rows * top * 4 // (3 * devices)

    order = list(range(0, columns, 2)) + list(range(columns - 1, 0, -2))
    forward = [(order[i], order[(i + 1) % columns]) for i in range(columns)]
    backward = [(b, a) for a, b in forward]
    column = lax.axis_index("exp")
    position = jnp.where(column % 2 == 0, column // 2, columns - 1 - column // 2)
    offsets = [0]
    for s in range(1, half):
        offsets += [-s, s]
    offsets += [half]
    source = jnp.asarray(order, jnp.int32)[(position + jnp.asarray(offsets, jnp.int32)) % columns]

    def ring_step(s, f, b):
        if s < half:
            return lax.ppermute(f, "exp", forward), lax.ppermute(b, "exp", backward)
        h = f.shape[0] // 2
        return lax.ppermute(f[:h], "exp", forward), lax.ppermute(b[h:], "exp", backward)

    def tie(arrays, deps):
        n = len(arrays)
        return list(lax.optimization_barrier(tuple(arrays) + tuple(deps))[:n])

    group = lax.axis_index("grp")
    plane, core = group // 2, group % 2
    swap_core = [(g, g ^ 1) for g in range(groups)]

    w = width // planes
    doubled = jnp.concatenate([grad_out, grad_out], axis=1)
    rolled = lax.dynamic_slice_in_dim(doubled, (plane + 1) * w, width, axis=1)
    far, near = rolled[:, : width - w], rolled[:, width - w :]

    def ready(a, deps):
        return tie([a], deps)[0]

    prob_expert, kept_route = routing(probs, expert_ids, serve_map, replica_pick, capacity)
    send = jnp.transpose(prob_expert, (1, 0, 2)).reshape(columns, rows * EXP_DEV).astype(BF)
    reorder = (source[:, None] == jnp.arange(columns, dtype=jnp.int32)[None, :]).astype(BF)

    def exchange(a):
        return lax.all_to_all(a, "exp", split_axis=0, concat_axis=0, tiled=True)

    shift = {"wide": 0, "near": half - 1}
    first = {"wide": jnp.concatenate([tokens, far], axis=1), "near": near}
    arrived = {name: [a] for name, a in first.items()}
    hand = {name: [a, a] for name, a in first.items()}
    fresh = [first["wide"]]
    hidden = []
    before = []
    stage_done = {}
    for i in range(1, half + 2):
        names = [name for name in shift if 1 <= i - shift[name] <= half]
        moving = [a for name in names for a in hand[name]]
        if before:
            moving = tie(moving, before)
        ran = []
        if i > 1:
            hidden.append(hidden_call(tie(fresh, before), w_gate, w_up))
            ran = list(hidden[-1])
            fresh = []
        if i == 3:
            prob_rows = dot(reorder, exchange(ready(send, before)), 1, 0)
            prob_rows = prob_rows.reshape(columns * rows, EXP_DEV)
            ran.append(prob_rows)
        done = []
        for j, name in enumerate(names):
            hand[name] = ring_step(i - shift[name], *moving[2 * j : 2 * j + 2])
            arrived[name] += hand[name]
            done += hand[name]
            if name == "wide":
                fresh += hand[name]
        before = done + ran + ([send] if i == 1 else [])
    x_all = arrived["wide"]
    hid, act, silu = [list(t) for t in zip(*hidden)]

    def near_step(s, before):
        hand["near"] = ring_step(s, *tie(hand["near"], before))
        arrived["near"] += hand["near"]
        return list(hand["near"])

    def part(s, lhs, which, rhs, p=None):
        start, pieces = lhs(s, which)
        return part_call([start], block, pieces, rhs, p)[0]

    def both_parts(lhs, rhs, p=None):
        (give_at, pieces), (keep_at, _) = lhs(0, 1 - core), lhs(0, core)
        return part_call([give_at, keep_at], block, pieces, rhs, p)

    def to_core(a):
        return lax.ppermute(a, "grp", swap_core)

    def to_plane(s, a):
        return lax.ppermute(a, "grp", [(g, (g + 2 * s) % groups) for g in range(groups)])

    def of_x(s, which):
        return (((plane + s) % planes) * 2 + which) * block, x_all

    def of_far(s, which):
        return width + ((s - 1) * 2 + which) * block, x_all

    def of_near(s, which):
        return which * block, near_all

    def add(*arrays):
        return sum(a.astype(F32) for a in arrays)

    given, mine, got = [], [], []
    for s in range(1, planes):
        hid_now = [ready(hid[0], before)] + hid[1:]
        given.append(part(s, of_far, 1 - core, [hid_now], prob_rows))
    done = near_step(3, before)
    before = done + given
    for s in range(1, planes):
        hid_now = [ready(hid[0], before)] + hid[1:]
        mine.append(part(s, of_far, core, [hid_now], prob_rows))
        got.append(to_core(ready(given[s - 1], before)))
    for s in range(4, half + 1):
        done = near_step(s, before if s == 4 else done)
    before = done + mine + got
    near_all = arrived["near"]

    h = block // 2
    mine = tie(mine, done)

    cuts = [lambda a: a[0, 0], lambda a: a[0, 1, :h], lambda a: a[0, 1, h:]]
    sums = [
        [add(cut(a), cut(b)).astype(BF) for a, b in zip(mine, got)] for cut in cuts
    ]

    def send_planes(sums, before):
        return [to_plane(s + 1, ready(a, before)) for s, a in enumerate(sums)]

    plane_ref = ready(plane.astype(jnp.int32).reshape(1), [a for t in sums for a in t])
    gg0, gg1, gu0, gu1, prob_grad = back_call(
        plane_ref, x_all, near_all, w_down, prob_rows, hid, act, silu, planes, 2
    )
    down0 = send_planes(sums[0], done)
    gg0, gg1, gu0, gu1, *down0 = tie([gg0, gg1, gu0, gu1] + down0, [])
    both = [[gg0, gg1], [gu0, gu1]]
    given = [part(s, of_x, 1 - core, both) for s in range(1, planes)]
    down1 = send_planes(sums[1], down0 + [gg0])
    gg0, *rest = tie([gg0] + given + down1, [])
    given, down1 = rest[: planes - 1], rest[planes - 1 :]
    both = [[gg0, gg1], [gu0, gu1]]
    mine_x = [part(s, of_x, core, both) for s in range(1, planes)]
    got_x = [to_core(a) for a in given]
    down2 = send_planes(sums[2], down1 + given)
    gg0, *rest = tie([gg0] + mine_x + got_x + down2, [])
    mine, got, down2 = rest[: planes - 1], rest[planes - 1 : -(planes - 1)], rest[1 - planes :]
    down = [[(a,) for a in down0], list(zip(down1, down2))]

    unit = block // 32
    stages = [
        [(0, 0, 0, 20)],
        [(0, 0, 20, 12), (0, 1, 0, 16)],
        [(0, 1, 16, 16), (1, 0, 0, 10)],
        [(1, 0, 10, 22), (1, 1, 0, 4)],
        [(1, 1, 4, 28)],
    ]
    theirs = {}

    def stage_sums(q, before):
        sums = []
        for i, m, first, n in stages[q] if q < len(stages) else []:
            here = slice(first * unit, (first + n) * unit)
            for a, b in zip(mine, got):
                a, b = tie([a, b], before)
                sums.append(add(a[i, m, here], b[i, m, here]).astype(BF))
        return sums

    def send_stage(q, sums):
        sent = []
        for t, (i, m, _, _) in enumerate(stages[q]):
            piece = sums[t * (planes - 1) : (t + 1) * (planes - 1)]
            piece = [to_plane(s + 1, a) for s, a in enumerate(piece)]
            theirs.setdefault((i, m), []).append(piece)
            sent += piece
        return sent

    def arrived_for(i, m):
        return list(zip(*theirs[i, m]))

    def step_back(b, f, before):
        b, f = tie([b, f], before)
        return lax.ppermute(b, "exp", backward), lax.ppermute(f, "exp", forward)

    sent = send_stage(0, stage_sums(0, []))
    extra = -(-columns * EXP_DEV // 128) * 128
    column_ref = column.astype(jnp.int32).reshape(1)
    cut = gg0.shape[0]
    late = input_call(
        column_ref, cut, ready(gg1, mine), gu1, prob_grad, w_gate, w_up, extra, False
    )
    sums = stage_sums(1, [late])
    late, gg0, *rest = tie([late, gg0] + sums + sent, [])
    sums, sent = rest[: len(sums)], rest[len(sums) :]
    at = {o: late[i * rows : (i + 1) * rows] for i, o in enumerate(offsets[-3:])}
    hr = rows // 2
    sent = send_stage(1, sums)
    sums = stage_sums(2, [late])
    b, f = step_back(at[half][:hr], at[half][hr:], [])
    rest = input_call(column_ref, 0, gg0, gu0, prob_grad, w_gate, w_up, extra, True)
    at.update({o: rest[i * rows : (i + 1) * rows] for i, o in enumerate(offsets[:-3])})
    done = sent + [rest]

    for q, s in enumerate(range(half - 1, 0, -1), 2):
        mine_b, mine_f = at[-s], at[s]
        if s == half - 1:
            mine_b = jnp.concatenate([mine_b[:hr] + b, mine_b[hr:]], axis=0)
            mine_f = jnp.concatenate([mine_f[:hr], mine_f[hr:] + f], axis=0)
        else:
            mine_b = mine_b + b
            mine_f = mine_f + f
        mine_b, mine_f, *before = tie([mine_b, mine_f] + sums + done, [])
        sums, done = before[: len(sums)], []
        if q < len(stages):
            done += send_stage(q, sums)
            sums = stage_sums(q + 1, before)
        b, f = step_back(mine_b, mine_f, [])
        if s == half - 1:
            both = [[ready(gg0, before), gg1], [gu0, gu1]]
            give_x, keep_x = both_parts(of_x, both)
            done += [give_x, keep_x]
        if s == half - 2:
            hid_now = [ready(hid[0], before)] + hid[1:]
            give_n, keep_n = both_parts(of_near, [hid_now], prob_rows)
            got_x = to_core(ready(give_x, before))
            done += [give_n, keep_n, got_x]
        if s == half - 3:
            got_n = to_core(ready(give_n, before))
            keep_x = ready(keep_x, before)
            grad_gate = finish_call(0, 0, keep_x, got_x, arrived_for(0, 0))
            grad_gate = finish_call(0, 1, keep_x, got_x, arrived_for(0, 1), grad_gate)
            grad_up = finish_call(1, 0, keep_x, got_x, arrived_for(1, 0))
            grad_down = finish_call(0, 0, ready(keep_n, before), got_n, down[0])
            grad_down = finish_call(0, 1, keep_n, got_n, down[1], grad_down)
            done += [grad_gate, grad_up, grad_down]
    at0, b, f, keep_x = tie([at[0], b, f, keep_x], [grad_down, grad_gate, grad_up])
    ret = add(*[a[:, width : width + columns * EXP_DEV] for a in (at0, b, f)]).astype(BF)
    grad_tokens = add(*[a[:, :width] for a in (at0, b, f)]).astype(BF)
    grad_up = finish_call(1, 1, keep_x, got_x, arrived_for(1, 1), grad_up, True)

    pick = expert_ids[:, :, None] == jnp.arange(columns * EXP_DEV, dtype=jnp.int32)
    grad_probs = jnp.sum(jnp.where(pick, ret.astype(F32)[:, None, :], 0.0), axis=2)
    grad_probs = jnp.where(kept_route, grad_probs, 0.0).astype(BF)
    return (grad_tokens, grad_probs, grad_gate, grad_up, grad_down)


def solution(mesh):
    rows = P(("grp", "exp"), None)
    weights = P("exp", None, None)
    out = P("exp", "grp", None)
    return jax.shard_map(
        body,
        mesh=mesh,
        in_specs=(rows, rows, rows, rows, P(), rows, weights, weights, weights),
        out_specs=(rows, rows, out, out, out),
        check_vma=False,
    )
```

```python
import functools

import jax
import jax.numpy as jnp
from jax import lax
from jax.experimental import pallas as pl
from jax.experimental.pallas import tpu as pltpu
from jax.sharding import PartitionSpec as P

EXP_DEV = 2
BF = jnp.bfloat16
F32 = jnp.float32


VMEM_BYTES = 56 * 2**20
ANY = pl.BlockSpec(memory_space=pl.ANY)


def dot(a, b, ca, cb):
    return lax.dot_general(a, b, (((ca,), (cb,)), ((), ())), preferred_element_type=F32)


def routing(probs, expert_ids, serve_map, replica_pick, capacity):
    groups, columns = serve_map.shape
    devices = groups * columns
    tokens = expert_ids.shape[0]
    member_of = serve_map.reshape(devices)
    serves_expert = 2 * (jnp.arange(devices, dtype=jnp.int32) % columns) + member_of
    same = (serve_map[:, None, :] == serve_map[None, :, :]).astype(jnp.int32)
    earlier = jnp.tril(jnp.ones((groups, groups), jnp.int32), -1)
    place = jnp.sum(same * earlier[:, :, None], axis=1).reshape(devices)
    count = jnp.sum(same, axis=1).reshape(devices)
    hit = (expert_ids[:, :, None] == serves_expert[None, None, :]) & (
        lax.rem(replica_pick[:, :, None], count[None, None, :]) == place[None, None, :]
    )
    chosen = jnp.sum(hit.astype(F32), axis=1)
    before = jnp.tril(jnp.ones((tokens, tokens), BF), -1)
    rank = dot(before, chosen.astype(BF), 1, 0)
    kept = (rank < capacity) & (chosen > 0)
    prob_dest = jnp.sum(jnp.where(hit, probs.astype(F32)[:, :, None], 0.0), axis=1)
    prob_dest = jnp.where(kept, prob_dest, 0.0).reshape(tokens, groups, columns)
    member = jnp.arange(EXP_DEV, dtype=jnp.int32)
    serving = (serve_map[:, :, None] == member[None, None, :]).astype(F32)
    prob_expert = jnp.sum(prob_dest[:, :, :, None] * serving[None], axis=1)
    kept_route = jnp.sum(jnp.where(hit & kept[:, None, :], 1.0, 0.0), axis=2) > 0
    return prob_expert, kept_route


def fetch(pieces, dst, sem, columns=None, at=0):
    copies = []
    row = 0
    for i, piece in enumerate(pieces):
        n = piece.shape[0]
        src = piece if columns is None else piece.at[:, columns]
        width = src.shape[1]
        copies.append(
            pltpu.make_async_copy(src, dst.at[pl.ds(row, n), pl.ds(at, width)], sem.at[i])
        )
        row += n
    for c in copies:
        c.start()
    return copies


def params(grid, nbytes):
    return dict(
        compiler_params=pltpu.CompilerParams(
            vmem_limit_bytes=min(VMEM_BYTES, int(nbytes) + 10 * 2**20),
            dimension_semantics=("arbitrary",) * grid,
        )
    )


def cost(flops, nbytes, trans=0):
    return pl.CostEstimate(flops=int(flops), bytes_accessed=int(nbytes), transcendentals=int(trans))


def hidden_kernel(count, nb, *refs):
    pieces = refs[:count]
    wg, wu, hid, act, silu_out, x, sem = refs[count:]

    @pl.when(pl.program_id(0) == 0)
    def _():
        for c in fetch(pieces, x, sem, columns=pl.ds(0, x.shape[1])):
            c.wait()

    for j in range(0, wg.shape[2], nb):
        cols = slice(j, j + nb)
        gate = jnp.dot(x[...], wg[0, :, cols], preferred_element_type=F32)
        up = jnp.dot(x[...], wu[0, :, cols], preferred_element_type=F32)
        sig = 1.0 / (1.0 + jnp.exp(-gate))
        silu = gate * sig
        hid[:, cols] = (silu * up).astype(BF)
        act[:, cols] = (up * sig * (1.0 + gate * (1.0 - sig))).astype(BF)
        silu_out[:, cols] = silu.astype(BF)


def hidden_call(pieces, w_gate, w_up, nb=256):
    rows = sum(a.shape[0] for a in pieces)
    n, width, ff = w_gate.shape
    ob = pl.BlockSpec((rows, ff), lambda m: (0, m))
    os = jax.ShapeDtypeStruct((rows, n * ff), BF)
    wb = pl.BlockSpec((1, width, ff), lambda m: (m, 0, 0))
    return pl.pallas_call(
        functools.partial(hidden_kernel, len(pieces), nb),
        grid=(n,),
        in_specs=[ANY] * len(pieces) + [wb, wb],
        out_specs=[ob] * 3,
        out_shape=[os] * 3,
        scratch_shapes=[pltpu.VMEM((rows, width), BF), pltpu.SemaphoreType.DMA((len(pieces),))],
        cost_estimate=cost(4 * rows * width * n * ff, 4 * n * width * ff + 8 * rows * ff * n),
        name="hidden",
        **params(1, VMEM_BYTES),
    )(*pieces, w_gate, w_up)


def back_kernel(counts, row_counts, late, planes, nb, plane_ref, *refs):
    na, nn = counts
    k = len(row_counts)
    pa, pb = refs[:na], refs[na : na + nn]
    refs = refs[na + nn :]
    acts = [refs[i * k : (i + 1) * k] for i in range(3)]
    wd, p = refs[3 * k : 3 * k + 2]
    gg0, gg1, gu0, gu1, pg, g, kept, sem, sem2, sem3 = refs[3 * k + 2 :]
    m = pl.program_id(0)
    w = g.shape[1] // planes
    ff = wd.shape[3]
    n_experts = kept.shape[2] // ff
    rest = g.shape[1] - w
    starts = [sum(row_counts[:i]) for i in range(k + 1)]
    chunks = [(0, k - late, gg0, gu0), (k - late, k, gg1, gu1)]

    def act_copies(lo, hi, e):
        cols = pl.ds(e * ff, ff)
        return [
            pltpu.make_async_copy(
                acts[t][i].at[:, cols],
                kept.at[t, pl.ds(starts[i], row_counts[i]), cols],
                sem3.at[t, i, e],
            )
            for i in range(lo, hi)
            for t in range(3)
        ]

    def row_copies(lo, hi):
        out = []
        row = 0
        for i in range(na):
            n = pa[i].shape[0]
            if starts[lo] <= row < starts[hi]:
                here = pl.ds(row, n)
                cols = pl.ds(pa[i].shape[1] - rest, rest)
                out.append(
                    pltpu.make_async_copy(
                        pa[i].at[:, cols], g.at[here, pl.ds(0, rest)], sem.at[i]
                    )
                )
                out.append(
                    pltpu.make_async_copy(pb[i], g.at[here, pl.ds(rest, w)], sem2.at[i])
                )
            row += n
        return out

    @pl.when(m == 0)
    def _():
        for lo, hi, _, _ in chunks:
            for c in row_copies(lo, hi) + act_copies(lo, hi, 0):
                c.start()
        for e in range(1, n_experts):
            for lo, hi, _, _ in chunks:
                for c in act_copies(lo, hi, e):
                    c.start()
        pg[...] = jnp.zeros_like(pg)

    for e in range(n_experts):

        @pl.when(m == e)
        def _(e=e):
            for lo, hi, gg, gu in chunks:
                waits = act_copies(lo, hi, e)
                if e == 0:
                    waits += row_copies(lo, hi)
                for c in waits:
                    c.wait()
                here = slice(starts[lo], starts[hi])
                n = starts[hi] - starts[lo]
                pv = p[here, e : e + 1]
                total = jnp.zeros((n, 1), F32)
                for j in range(0, ff, nb):
                    cols = slice(j, j + nb)
                    from_cols = slice(e * ff + j, e * ff + j + nb)
                    back = jnp.zeros((n, nb), F32)
                    for s in range(planes):
                        at = lax.rem(plane_ref[0] + 1 + s, planes)
                        back += jnp.dot(
                            g[here, s * w : (s + 1) * w],
                            wd[0, at, :, cols],
                            preferred_element_type=F32,
                        )
                    total += jnp.sum(
                        back * kept[0, here, from_cols].astype(F32), axis=1, keepdims=True
                    )
                    back = (back * pv).astype(BF)
                    gg[:, cols] = back * kept[1, here, from_cols]
                    gu[:, cols] = back * kept[2, here, from_cols]
                lane = lax.broadcasted_iota(jnp.int32, (n, pg.shape[1]), 1) == e
                pg[here, :] += jnp.where(lane, total, 0.0)


def back_call(plane, pa, pb, w_down, p, hid, act, silu, planes, late, nb=256):
    rows = sum(a.shape[0] for a in pa)
    n, width, ff = w_down.shape
    w = width // planes
    row_counts = [a.shape[0] for a in hid]
    k = len(row_counts)
    split = [sum(row_counts[: k - late]), sum(row_counts[k - late :])]
    ob = [pl.BlockSpec((r, ff), lambda m, *_: (0, m)) for r in split]
    os = [jax.ShapeDtypeStruct((r, n * ff), BF) for r in split]
    wb = pl.BlockSpec((1, planes, w, ff), lambda m, *_: (m, 0, 0, 0))
    return pl.pallas_call(
        functools.partial(back_kernel, (len(pa), len(pb)), row_counts, late, planes, nb),
        grid_spec=pltpu.PrefetchScalarGridSpec(
            num_scalar_prefetch=1,
            grid=(n,),
            in_specs=[ANY] * (len(pa) + len(pb) + 3 * k)
            + [wb, pl.BlockSpec((rows, n), lambda m, *_: (0, 0))],
            out_specs=ob + ob + [pl.BlockSpec((rows, n), lambda m, *_: (0, 0))],
            scratch_shapes=[
                pltpu.VMEM((rows, width), BF),
                pltpu.VMEM((3, rows, n * ff), BF),
                pltpu.SemaphoreType.DMA((len(pa),)),
                pltpu.SemaphoreType.DMA((len(pb),)),
                pltpu.SemaphoreType.DMA((3, k, n)),
            ],
        ),
        out_shape=os + os + [jax.ShapeDtypeStruct((rows, n), F32)],
        cost_estimate=cost(2 * rows * width * n * ff, 2 * n * width * ff + 14 * rows * ff * n),
        name="back",
        **params(1, VMEM_BYTES),
    )(plane, *pa, *pb, *hid, *act, *silu, w_down.reshape(n, planes, w, ff), p)


def part_kernel(count, row_counts, arrays, scale, sides, start_ref, *refs):
    pieces = refs[:count]
    refs = refs[count:]
    if scale:
        p, refs = refs[0], refs[1:]
    k = len(row_counts)
    rhs_in = [refs[i * k : (i + 1) * k] for i in range(arrays)]
    outs = refs[arrays * k : arrays * k + sides]
    lhs, rhs, sem, sem2 = refs[arrays * k + sides :]
    block = lhs.shape[2]
    ff = outs[0].shape[3]
    n_experts = rhs.shape[2] // ff
    m = pl.program_id(0)

    def rhs_copies(e):
        copies = []
        for i in range(arrays):
            row = 0
            for j, n in enumerate(row_counts):
                copies.append(
                    pltpu.make_async_copy(
                        rhs_in[i][j].at[:, pl.ds(e * ff, ff)],
                        rhs.at[i, pl.ds(row, n), pl.ds(e * ff, ff)],
                        sem2.at[i, j, e],
                    )
                )
                row += n
        return copies

    @pl.when(m == 0)
    def _():
        first = []
        for q in range(sides):
            cols = pl.ds(pl.multiple_of(start_ref[q] * 128, 128), block)
            first += fetch(pieces, lhs.at[q], sem.at[q], columns=cols)
        for e in range(n_experts):
            for c in rhs_copies(e):
                c.start()
        for c in first:
            c.wait()

    for e in range(n_experts):

        @pl.when(m == e)
        def _(e=e):
            for c in rhs_copies(e):
                c.wait()
            for i in range(arrays):
                r = rhs[i, :, e * ff : (e + 1) * ff]
                if scale:
                    r = r * p[:, e : e + 1].astype(BF)
                for q in range(sides):
                    outs[q][i, 0] = lax.dot_general(
                        lhs[q], r, (((0,), (0,)), ((), ())), preferred_element_type=F32
                    ).astype(BF)


def part_call(starts, block, pieces, rhs, p=None):
    sides = len(starts)
    rows = sum(a.shape[0] for a in pieces)
    n = EXP_DEV
    k = len(rhs)
    ff = rhs[0][0].shape[1] // n
    row_counts = [a.shape[0] for a in rhs[0]]
    scale = [] if p is None else [p]
    flat_rhs = [a for r in rhs for a in r]
    nbytes = 2 * rows * (sides * block + k * n * ff) + 4 * sides * k * block * ff
    nbytes += 8 * block * ff + 1024 * rows
    return pl.pallas_call(
        functools.partial(part_kernel, len(pieces), row_counts, k, bool(scale), sides),
        grid_spec=pltpu.PrefetchScalarGridSpec(
            num_scalar_prefetch=1,
            grid=(n,),
            in_specs=[ANY] * len(pieces)
            + [pl.BlockSpec((rows, n), lambda m, *_: (0, 0))] * len(scale)
            + [ANY] * len(flat_rhs),
            out_specs=[pl.BlockSpec((k, 1, block, ff), lambda m, *_: (0, m, 0, 0))] * sides,
            scratch_shapes=[
                pltpu.VMEM((sides, rows, block), BF),
                pltpu.VMEM((k, rows, n * ff), BF),
                pltpu.SemaphoreType.DMA((sides, len(pieces))),
                pltpu.SemaphoreType.DMA((k, len(row_counts), n)),
            ],
        ),
        out_shape=[jax.ShapeDtypeStruct((k, n, block, ff), BF)] * sides,
        cost_estimate=cost(
            2 * rows * block * n * ff * k * sides,
            2 * rows * (sides * block + k * n * ff) + 2 * sides * k * n * block * ff,
        ),
        name="part",
        **params(1, nbytes if sides > 1 else VMEM_BYTES),
    )(jnp.stack(starts).astype(jnp.int32) // 128, *pieces, *scale, *flat_rhs)


def input_kernel(first_row, column_ref, gg, gu, pg, wg, wu, out):
    ff = wg.shape[2]
    width = wg.shape[1] * pl.num_programs(0)
    c = (((1,), (1,)), ((), ()))
    acc = lax.dot_general(gg[:, :ff], wg[0], c, preferred_element_type=F32)
    acc += lax.dot_general(gg[:, ff:], wg[1], c, preferred_element_type=F32)
    acc += lax.dot_general(gu[:, :ff], wu[0], c, preferred_element_type=F32)
    acc += lax.dot_general(gu[:, ff:], wu[1], c, preferred_element_type=F32)
    nb = wg.shape[1]
    j = pl.program_id(0)
    out[:, pl.ds(pl.multiple_of(j * nb, nb), nb)] = acc.astype(BF)

    @pl.when(j == 0)
    def _():
        rows, extra = out.shape[0], out.shape[1] - width
        lane = lax.broadcasted_iota(jnp.int32, (rows, extra), 1)
        total = jnp.zeros((rows, extra), F32)
        for m in range(EXP_DEV):
            value = pg[first_row : first_row + rows, m : m + 1]
            total = jnp.where(lane == column_ref[0] * EXP_DEV + m, value, total)
        out[:, width:] = total.astype(BF)


def input_call(column, first_row, gg, gu, prob_grad, w_gate, w_up, extra, ahead, nb=512):
    rows = gg.shape[0]
    n, width, ff = w_gate.shape
    wb = pl.BlockSpec((n, nb, ff), lambda j, *_: (0, j, 0))
    gb = pl.BlockSpec((rows, n * ff), lambda j, *_: (0, 0))
    nbytes = 4 * (2 * rows * n * ff + rows * (width + extra) + 2 * n * nb * ff) + 8 * rows * nb
    return pl.pallas_call(
        functools.partial(input_kernel, first_row),
        grid_spec=pltpu.PrefetchScalarGridSpec(
            num_scalar_prefetch=1,
            grid=(width // nb,),
            in_specs=[gb, gb, pl.BlockSpec(prob_grad.shape, lambda j, *_: (0, 0)), wb, wb],
            out_specs=pl.BlockSpec((rows, width + extra), lambda j, *_: (0, 0)),
        ),
        out_shape=jax.ShapeDtypeStruct((rows, width + extra), BF),
        cost_estimate=cost(
            4 * rows * width * n * ff, 4 * n * width * ff + 4 * rows * ff * n + 2 * rows * width
        ),
        name="input",
        **params(1, nbytes if ahead else VMEM_BYTES),
    )(column, gg, gu, prob_grad, w_gate, w_up)


def finish_kernel(into, counts, steps, *refs):
    refs = refs[into:]
    rb = refs[-1].shape[1]
    r = pl.program_id(0)

    for k in range(steps):

        @pl.when(r == k)
        def _(k=k):
            total = refs[0][0, 0].astype(F32) + refs[1][0, 0].astype(F32)
            at = 2
            for sizes in counts:
                rows, row = [], 0
                for n in sizes:
                    lo, hi = max(row, k * rb), min(row + n, (k + 1) * rb)
                    if lo < hi:
                        rows.append(refs[at][lo - row : hi - row])
                    row += n
                    at += 1
                one = rows[0] if len(rows) == 1 else jnp.concatenate(rows, axis=0)
                total = total + one.astype(F32)
            refs[-1][0] = total


def finish_call(i, m, mine, got, theirs, into=None, last=False, steps=2):
    _, n, block, ff = mine.shape
    rb = block // steps
    stacked = pl.BlockSpec((1, 1, rb, ff), lambda r: (i, m, r, 0))
    extra = [] if into is None else [into]
    arrays = [a for t in theirs for a in t]
    return pl.pallas_call(
        functools.partial(
            finish_kernel, len(extra), [[a.shape[0] for a in t] for t in theirs], steps
        ),
        grid=(steps,),
        in_specs=[ANY] * len(extra)
        + [stacked, stacked]
        + [pl.BlockSpec(a.shape, lambda r: (0, 0)) for a in arrays],
        out_specs=pl.BlockSpec((1, rb, ff), lambda r: (m, r, 0)),
        out_shape=jax.ShapeDtypeStruct((n, block, ff), F32),
        input_output_aliases={0: 0} if extra else {},
        cost_estimate=cost(3 * block * ff, 10 * block * ff),
        name="finish",
        **params(1, VMEM_BYTES if last else 24 * block * ff),
    )(*extra, mine, got, *arrays)


def body(tokens, grad_out, probs, expert_ids, serve_map, replica_pick, w_gate, w_up, w_down):
    groups = lax.axis_size("grp")
    columns = lax.axis_size("exp")
    devices = groups * columns
    planes = groups // 2
    half = columns // 2
    rows, width = tokens.shape
    top = expert_ids.shape[1]
    block = width // groups
    capacity = rows * top * 4 // (3 * devices)

    order = list(range(0, columns, 2)) + list(range(columns - 1, 0, -2))
    forward = [(order[i], order[(i + 1) % columns]) for i in range(columns)]
    backward = [(b, a) for a, b in forward]
    column = lax.axis_index("exp")
    position = jnp.where(column % 2 == 0, column // 2, columns - 1 - column // 2)
    offsets = [0]
    for s in range(1, half):
        offsets += [-s, s]
    offsets += [half]
    source = jnp.asarray(order, jnp.int32)[(position + jnp.asarray(offsets, jnp.int32)) % columns]

    def ring_step(s, f, b):
        if s < half:
            return lax.ppermute(f, "exp", forward), lax.ppermute(b, "exp", backward)
        h = f.shape[0] // 2
        return lax.ppermute(f[:h], "exp", forward), lax.ppermute(b[h:], "exp", backward)

    def tie(arrays, deps):
        n = len(arrays)
        return list(lax.optimization_barrier(tuple(arrays) + tuple(deps))[:n])

    group = lax.axis_index("grp")
    plane, core = group // 2, group % 2
    swap_core = [(g, g ^ 1) for g in range(groups)]

    w = width // planes
    doubled = jnp.concatenate([grad_out, grad_out], axis=1)
    rolled = lax.dynamic_slice_in_dim(doubled, (plane + 1) * w, width, axis=1)
    far, near = rolled[:, : width - w], rolled[:, width - w :]

    def ready(a, deps):
        return tie([a], deps)[0]

    prob_expert, kept_route = routing(probs, expert_ids, serve_map, replica_pick, capacity)
    send = jnp.transpose(prob_expert, (1, 0, 2)).reshape(columns, rows * EXP_DEV).astype(BF)
    reorder = (source[:, None] == jnp.arange(columns, dtype=jnp.int32)[None, :]).astype(BF)

    def exchange(a):
        return lax.all_to_all(a, "exp", split_axis=0, concat_axis=0, tiled=True)

    shift = {"wide": 0, "near": half - 1}
    first = {"wide": jnp.concatenate([tokens, far], axis=1), "near": near}
    arrived = {name: [a] for name, a in first.items()}
    hand = {name: [a, a] for name, a in first.items()}
    fresh = [first["wide"]]
    hidden = []
    before = []
    stage_done = {}
    for i in range(1, half + 2):
        names = [name for name in shift if 1 <= i - shift[name] <= half]
        moving = [a for name in names for a in hand[name]]
        if before:
            moving = tie(moving, before)
        ran = []
        if i > 1:
            hidden.append(hidden_call(tie(fresh, before), w_gate, w_up))
            ran = list(hidden[-1])
            fresh = []
        if i == 3:
            prob_rows = dot(reorder, exchange(ready(send, before)), 1, 0)
            prob_rows = prob_rows.reshape(columns * rows, EXP_DEV)
            ran.append(prob_rows)
        done = []
        for j, name in enumerate(names):
            hand[name] = ring_step(i - shift[name], *moving[2 * j : 2 * j + 2])
            arrived[name] += hand[name]
            done += hand[name]
            if name == "wide":
                fresh += hand[name]
        before = done + ran + ([send] if i == 1 else [])
    x_all = arrived["wide"]
    hid, act, silu = [list(t) for t in zip(*hidden)]

    def near_step(s, before):
        hand["near"] = ring_step(s, *tie(hand["near"], before))
        arrived["near"] += hand["near"]
        return list(hand["near"])

    def part(s, lhs, which, rhs, p=None):
        start, pieces = lhs(s, which)
        return part_call([start], block, pieces, rhs, p)[0]

    def both_parts(lhs, rhs, p=None):
        (give_at, pieces), (keep_at, _) = lhs(0, 1 - core), lhs(0, core)
        return part_call([give_at, keep_at], block, pieces, rhs, p)

    def to_core(a):
        return lax.ppermute(a, "grp", swap_core)

    def to_plane(s, a):
        return lax.ppermute(a, "grp", [(g, (g + 2 * s) % groups) for g in range(groups)])

    def of_x(s, which):
        return (((plane + s) % planes) * 2 + which) * block, x_all

    def of_far(s, which):
        return width + ((s - 1) * 2 + which) * block, x_all

    def of_near(s, which):
        return which * block, near_all

    def add(*arrays):
        return sum(a.astype(F32) for a in arrays)

    given, mine, got = [], [], []
    for s in range(1, planes):
        hid_now = [ready(hid[0], before)] + hid[1:]
        given.append(part(s, of_far, 1 - core, [hid_now], prob_rows))
    done = near_step(3, before)
    before = done + given
    for s in range(1, planes):
        hid_now = [ready(hid[0], before)] + hid[1:]
        mine.append(part(s, of_far, core, [hid_now], prob_rows))
        got.append(to_core(ready(given[s - 1], before)))
    for s in range(4, half + 1):
        done = near_step(s, before if s == 4 else done)
    before = done + mine + got
    near_all = arrived["near"]

    h = block // 2
    mine = tie(mine, done)

    cuts = [lambda a: a[0, 0], lambda a: a[0, 1, :h], lambda a: a[0, 1, h:]]
    sums = [
        [add(cut(a), cut(b)).astype(BF) for a, b in zip(mine, got)] for cut in cuts
    ]

    def send_planes(sums, before):
        return [to_plane(s + 1, ready(a, before)) for s, a in enumerate(sums)]

    plane_ref = ready(plane.astype(jnp.int32).reshape(1), [a for t in sums for a in t])
    gg0, gg1, gu0, gu1, prob_grad = back_call(
        plane_ref, x_all, near_all, w_down, prob_rows, hid, act, silu, planes, 2
    )
    down0 = send_planes(sums[0], done)
    gg0, gg1, gu0, gu1, *down0 = tie([gg0, gg1, gu0, gu1] + down0, [])
    both = [[gg0, gg1], [gu0, gu1]]
    given = [part(s, of_x, 1 - core, both) for s in range(1, planes)]
    down1 = send_planes(sums[1], down0 + [gg0])
    gg0, *rest = tie([gg0] + given + down1, [])
    given, down1 = rest[: planes - 1], rest[planes - 1 :]
    both = [[gg0, gg1], [gu0, gu1]]
    mine_x = [part(s, of_x, core, both) for s in range(1, planes)]
    got_x = [to_core(a) for a in given]
    down2 = send_planes(sums[2], down1 + given)
    gg0, *rest = tie([gg0] + mine_x + got_x + down2, [])
    mine, got, down2 = rest[: planes - 1], rest[planes - 1 : -(planes - 1)], rest[1 - planes :]
    down = [[(a,) for a in down0], list(zip(down1, down2))]

    unit = block // 32
    stages = [
        [(0, 0, 0, 20)],
        [(0, 0, 20, 12), (0, 1, 0, 16)],
        [(0, 1, 16, 16), (1, 0, 0, 10)],
        [(1, 0, 10, 22), (1, 1, 0, 4)],
        [(1, 1, 4, 28)],
    ]
    theirs = {}

    def stage_sums(q, before):
        sums = []
        for i, m, first, n in stages[q] if q < len(stages) else []:
            here = slice(first * unit, (first + n) * unit)
            for a, b in zip(mine, got):
                a, b = tie([a, b], before)
                sums.append(add(a[i, m, here], b[i, m, here]).astype(BF))
        return sums

    def send_stage(q, sums):
        sent = []
        for t, (i, m, _, _) in enumerate(stages[q]):
            piece = sums[t * (planes - 1) : (t + 1) * (planes - 1)]
            piece = [to_plane(s + 1, a) for s, a in enumerate(piece)]
            theirs.setdefault((i, m), []).append(piece)
            sent += piece
        return sent

    def arrived_for(i, m):
        return list(zip(*theirs[i, m]))

    def step_back(b, f, before):
        b, f = tie([b, f], before)
        return lax.ppermute(b, "exp", backward), lax.ppermute(f, "exp", forward)

    sent = send_stage(0, stage_sums(0, []))
    extra = -(-columns * EXP_DEV // 128) * 128
    column_ref = column.astype(jnp.int32).reshape(1)
    cut = gg0.shape[0]
    late = input_call(
        column_ref, cut, ready(gg1, mine), gu1, prob_grad, w_gate, w_up, extra, False
    )
    sums = stage_sums(1, [late])
    late, gg0, *rest = tie([late, gg0] + sums + sent, [])
    sums, sent = rest[: len(sums)], rest[len(sums) :]
    at = {o: late[i * rows : (i + 1) * rows] for i, o in enumerate(offsets[-3:])}
    hr = rows // 2
    sent = send_stage(1, sums)
    sums = stage_sums(2, [late])
    b, f = step_back(at[half][:hr], at[half][hr:], [])
    rest = input_call(column_ref, 0, gg0, gu0, prob_grad, w_gate, w_up, extra, True)
    at.update({o: rest[i * rows : (i + 1) * rows] for i, o in enumerate(offsets[:-3])})
    done = sent + [rest]

    for q, s in enumerate(range(half - 1, 0, -1), 2):
        mine_b, mine_f = at[-s], at[s]
        if s == half - 1:
            mine_b = jnp.concatenate([mine_b[:hr] + b, mine_b[hr:]], axis=0)
            mine_f = jnp.concatenate([mine_f[:hr], mine_f[hr:] + f], axis=0)
        else:
            mine_b = mine_b + b
            mine_f = mine_f + f
        mine_b, mine_f, *before = tie([mine_b, mine_f] + sums + done, [])
        sums, done = before[: len(sums)], []
        if q < len(stages):
            done += send_stage(q, sums)
            sums = stage_sums(q + 1, before) if q > 2 else []
        b, f = step_back(mine_b, mine_f, [])
        if s == half - 1:
            both = [[ready(gg0, before), gg1], [gu0, gu1]]
            give_x, keep_x = both_parts(of_x, both)
            done += [give_x, keep_x]
            sums = stage_sums(q + 1, [keep_x])
        if s == half - 2:
            hid_now = [ready(hid[0], before)] + hid[1:]
            give_n, keep_n = both_parts(of_near, [hid_now], prob_rows)
            got_x = to_core(ready(give_x, before))
            done += [give_n, keep_n, got_x]
        if s == half - 3:
            got_n = to_core(ready(give_n, before))
            keep_x = ready(keep_x, before)
            grad_gate = finish_call(0, 0, keep_x, got_x, arrived_for(0, 0))
            grad_gate = finish_call(0, 1, keep_x, got_x, arrived_for(0, 1), grad_gate)
            grad_up = finish_call(1, 0, keep_x, got_x, arrived_for(1, 0))
            grad_down = finish_call(0, 0, ready(keep_n, before), got_n, down[0])
            grad_down = finish_call(0, 1, keep_n, got_n, down[1], grad_down)
            done += [grad_gate, grad_up, grad_down]
    at0, b, f, keep_x = tie([at[0], b, f, keep_x], [grad_down, grad_gate, grad_up])
    ret = add(*[a[:, width : width + columns * EXP_DEV] for a in (at0, b, f)]).astype(BF)
    grad_tokens = add(*[a[:, :width] for a in (at0, b, f)]).astype(BF)
    grad_up = finish_call(1, 1, keep_x, got_x, arrived_for(1, 1), grad_up, True)

    pick = expert_ids[:, :, None] == jnp.arange(columns * EXP_DEV, dtype=jnp.int32)
    grad_probs = jnp.sum(jnp.where(pick, ret.astype(F32)[:, None, :], 0.0), axis=2)
    grad_probs = jnp.where(kept_route, grad_probs, 0.0).astype(BF)
    return (grad_tokens, grad_probs, grad_gate, grad_up, grad_down)


def solution(mesh):
    rows = P(("grp", "exp"), None)
    weights = P("exp", None, None)
    out = P("exp", "grp", None)
    return jax.shard_map(
        body,
        mesh=mesh,
        in_specs=(rows, rows, rows, rows, P(), rows, weights, weights, weights),
        out_specs=(rows, rows, out, out, out),
        check_vma=False,
    )
```
